512 devices in a mesh: row: 32 (over x_hi, z, core), col: 16 (over y, x_lo).
Axes of the slice: x: 4 (x_hi: 2, x_lo: 2; x = x_hi * 2 + x_lo), y: 8, z: 8, core: 2. Of those that a mesh axis runs over, the one named last changes fastest.
Arguments:
- tensor: float32 [8, 4096, 4096], P(None, 'row', 'col'), may hold values from -6 to 6
- factor_a: float32 [32, 4096], P(None, 'row'), as said below
- factor_b: float32 [32, 4096], P(None, 'col'), as said below
- factor_c: float32 [32, 8], replicated, may hold values from -2.5 to 2.5
Outputs:
- new_a: float32 [32, 4096], P(None, 'row')
- new_b: float32 [32, 4096], P(None, 'col')
- new_c: float32 [32, 8], replicated
The draws below stay inside these ranges and needn't reach their ends.
Inputs may be any that keep to these rules, and one draw needn't show every extreme that they name: factor_a's scale differs from index to index. factor_b's scale differs from index to index.
All inputs are finite; a program needn't handle non-finite values.
Results may differ from the reference program's by a relative error of at most 0.0003.
Values sent between devices are 32-bit elements; how exact they have to be, the bound alone decides.
No kernel may reach another device: no remote copies, remote signals or barrier semaphores. Data moves between devices by JAX's collectives and lax.ppermute only.
A program may use at most 64 MiB of HBM per device.

```python
import jax
import jax.numpy as jnp
from jax import lax

R = 32
K = 8
ITERS = 6
NI = 4096
NJ = 4096


def scaled_factor(key, rows, length, spread):
    scale_key, noise_key = jax.random.split(key, 2)
    scales = jnp.exp(jax.random.uniform(scale_key, (1, length), jnp.float32) * jnp.log(spread))
    noise = jax.random.normal(noise_key, (rows, length), jnp.float32)
    return noise * scales / (0.5 * spread * jnp.sqrt(length * 1.0))


def draw_factor_a(key, part):
    key = jax.random.fold_in(key, 11)
    return scaled_factor(key, R, NI, 10.0)


def draw_factor_b(key, part):
    key = jax.random.fold_in(key, 23)
    return scaled_factor(key, R, NJ, 10.0)


def block_scale(own_key, dims, pieces, smallest, largest):
    def one(axis_at, blocks):
        steps = jax.random.uniform(jax.random.fold_in(jax.random.fold_in(own_key, 6), axis_at), (blocks,), jnp.float32, smallest / len(pieces), largest / len(pieces))
        return jnp.repeat(jnp.exp(steps), dims[axis_at] // blocks).reshape((-1,) + (1,) * (len(dims) - axis_at - 1))

    level = one(*pieces[0])
    for cut in pieces[1:]:
        level = level * one(*cut)
    return level


def gaussian(key, shape, width, bound, cuts=(), dtype=jnp.bfloat16):
    drawn = width * jax.random.normal(key, shape, jnp.float32)
    if cuts:
        drawn = drawn * block_scale(key, shape, cuts, -0.22, 0.18)
    return jnp.clip(drawn, -bound, bound).astype(dtype)


def setup_inputs(seed: int = 0) -> dict:
    arg_keys = jax.random.split(jax.random.key(seed), 5)
    tensor = gaussian(arg_keys[0], (K, NI, NJ), 1.0, 6.0, ((1, 32), (2, 16)), jnp.float32)
    factor_a = draw_factor_a(jax.random.fold_in(arg_keys[4], 71), 0)
    factor_b = draw_factor_b(jax.random.fold_in(arg_keys[4], 71), 0)
    factor_c = gaussian(arg_keys[3], (R, K), 0.35, 2.5, (), jnp.float32)
    return dict(tensor=tensor, factor_a=factor_a, factor_b=factor_b, factor_c=factor_c)


HP = lax.Precision.HIGHEST

def gram(factor):
    return jnp.dot(factor, factor.T, precision=HP)

def inverse_norm(matrix):
    return 1.0 / jnp.sqrt(jnp.sum(matrix * matrix) + 1e-06)

def reference(tensor, factor_a, factor_b, factor_c):
    fa, fb, fc = (factor_a, factor_b, factor_c)
    for step in range(ITERS):
        gram_a, gram_b, gram_c = (gram(fa), gram(fb), gram(fc))
        part_y = jnp.einsum('kij,rj->kri', tensor, fb, precision=HP)
        mode_a = jnp.einsum('rk,kri->ri', fc, part_y, precision=HP)
        mode_c = jnp.einsum('kri,ri->rk', part_y, fa, precision=HP)
        part_z = jnp.einsum('kij,ri->krj', tensor, fa, precision=HP)
        mode_b = jnp.einsum('rk,krj->rj', fc, part_z, precision=HP)
        h_a, h_b, h_c = (gram_b * gram_c, gram_a * gram_c, gram_a * gram_b)
        next_a = fa - inverse_norm(h_a) * (jnp.dot(h_a, fa, precision=HP) - mode_a)
        next_b = fb - inverse_norm(h_b) * (jnp.dot(h_b, fb, precision=HP) - mode_b)
        next_c = fc - inverse_norm(h_c) * (jnp.dot(h_c, fc, precision=HP) - mode_c)
        fa, fb, fc = (next_a, next_b, next_c)
    return (fa, fb, fc)
```

```python
import jax
import jax.numpy as jnp
from jax import lax
from jax.sharding import Mesh, PartitionSpec as P

ITERS = 6

HP = lax.Precision.HIGHEST


def gram(factor):
    return jnp.dot(factor, factor.T, precision=HP)


def pack(square):
    n = square.shape[1]
    rows = square.reshape(4, 8, n).transpose(1, 0, 2).reshape(8, 4 * n)
    return jnp.pad(rows, ((0, 0), (0, 128 - 4 * n)))


def unpack(rows, n):
    return rows[:, : 4 * n].reshape(8, 4, n).transpose(1, 0, 2).reshape(32, n)


def inverse_norm(matrix):
    return 1.0 / jnp.sqrt(jnp.sum(matrix * matrix) + 1e-06)


def descend(factor, hessian, contraction):
    return factor - inverse_norm(hessian) * (jnp.dot(hessian, factor, precision=HP) - contraction)


def sum_over(block, axis, size):
    copies = jnp.broadcast_to(block[None], (size,) + block.shape)
    return lax.all_to_all(copies, axis, 0, 0).sum(0)


def shards(tensor, factor_a, factor_b, factor_c):
    fa, fb, fc = (factor_a, factor_b, factor_c)
    x_lo = lax.axis_index("x_lo")
    chip = lax.axis_index("x_hi") * 2 + lax.axis_index("core")
    for step in range(ITERS):
        gram_c = gram(fc)
        part_y = jnp.einsum("kij,rj->kri", tensor, fb, precision=HP)
        part_z = jnp.einsum("kij,ri->krj", tensor, fa, precision=HP)
        part_a = jnp.einsum("rk,kri->ri", fc, part_y, precision=HP)
        part_c = jnp.einsum("kri,ri->rk", part_y, fa, precision=HP)
        part_b = jnp.einsum("rk,krj->rj", fc, part_z, precision=HP)
        for_row = jnp.concatenate([part_b[:, :128], part_b[:, 128:], pack(gram(fa))], 0)
        for_col = jnp.concatenate([part_a, pack(gram(fb)), jnp.zeros((32, 128), jnp.float32)], 0)
        same = jnp.arange(2)[:, None, None] == x_lo
        pair = jnp.where(same, for_row[None], for_col[None])
        pair = jnp.concatenate([pair, jnp.broadcast_to(pack(part_c)[None], (2, 8, 128))], 1)
        sent = jnp.broadcast_to(pair[:, None], (2, 4, 80, 128)).reshape(8, 80, 128)
        got = lax.all_to_all(sent, ("x_lo", "x_hi", "core"), 0, 0)
        sum_c = got[:, 72:].sum(0)
        got = got.reshape(2, 4, 80, 128)
        sum_row = lax.dynamic_index_in_dim(got, x_lo, 0, False)[:, :72].sum(0)
        other = lax.dynamic_index_in_dim(got, 1 - x_lo, 0, False)
        sum_col = for_col[:40] + lax.dynamic_index_in_dim(other, chip, 0, False)[:40]
        sum_row = sum_over(jnp.concatenate([sum_row, sum_c], 0), "z", 8)
        sum_col = sum_over(jnp.concatenate([sum_col, sum_row[72:]], 0), "y", 8)
        mode_b = jnp.concatenate([sum_row[:32], sum_row[32:64]], 1)
        gram_a = unpack(sum_row[64:72], 32)
        mode_a = sum_col[:32]
        gram_b = unpack(sum_col[32:40], 32)
        mode_c = unpack(sum_col[40:48], 8)
        next_a = descend(fa, gram_b * gram_c, mode_a)
        next_b = descend(fb, gram_a * gram_c, mode_b)
        next_c = descend(fc, gram_a * gram_b, mode_c)
        fa, fb, fc = (next_a, next_b, next_c)
    return (fa, fb, fc)


def solution(mesh):
    rows, cols = mesh.devices.shape
    devices = mesh.devices.reshape(2, rows // 4, 2, cols // 2, 2)
    fine = Mesh(devices, ("x_hi", "z", "core", "y", "x_lo"))
    row, col = (("x_hi", "z", "core"), ("y", "x_lo"))
    in_specs = (P(None, row, col), P(None, row), P(None, col), P())
    out_specs = (P(None, row), P(None, col), P())
    return jax.shard_map(shards, mesh=fine, in_specs=in_specs, out_specs=out_specs, check_vma=False)
```

```python
import jax
import jax.numpy as jnp
from jax import lax
from jax.sharding import Mesh, PartitionSpec as P

ITERS = 6

HP = lax.Precision.HIGHEST
NEAR = ("x_lo", "x_hi", "core")


def gram(factor):
    return jnp.dot(factor, factor.T, precision=HP)


def inverse_norm(matrix):
    return 1.0 / jnp.sqrt(jnp.sum(matrix * matrix) + 1e-06)


def descend(factor, hessian, contraction):
    return factor - inverse_norm(hessian) * (jnp.dot(hessian, factor, precision=HP) - contraction)


def sum_over(block, axis, size):
    copies = jnp.broadcast_to(block[None], (size,) + block.shape)
    return lax.all_to_all(copies, axis, 0, 0).sum(0)


def tile(*pieces):
    return jnp.concatenate(pieces + (jnp.zeros((8, 128 - sum(p.shape[1] for p in pieces)), jnp.float32),), 1)


def row_message(part_b, gram_a, part_c, quarter):
    rows = slice(8 * quarter, 8 * quarter + 8)
    gap = jnp.zeros((8, 32), jnp.float32)
    return jnp.concatenate([part_b[rows, :128], part_b[rows, 128:], tile(gram_a[rows], gap, part_c[rows])], 0)


def col_message(part_a, gram_b, part_c, half, quarter):
    rows = slice(16 * half, 16 * half + 16)
    rows_b = gram_b[rows]
    part_c = part_c[8 * quarter : 8 * quarter + 8]
    return jnp.concatenate([part_a[rows], tile(rows_b[:8], rows_b[8:], part_c)], 0)


def shards(tensor, factor_a, factor_b, factor_c):
    fa, fb, fc = (factor_a, factor_b, factor_c)
    x_lo = lax.axis_index("x_lo")
    chip = lax.axis_index("x_hi") * 2 + lax.axis_index("core")
    same = jnp.arange(2)[:, None, None, None] == x_lo
    lane = jnp.arange(128)[None, :]
    lanes_c = (jnp.arange(24)[:, None] >= 16) & (lane >= 64)
    for step in range(ITERS):
        gram_a, gram_b, gram_c = (gram(fa), gram(fb), gram(fc))
        part_y = jnp.einsum("kij,rj->kri", tensor, fb, precision=HP)
        part_z = jnp.einsum("kij,ri->krj", tensor, fa, precision=HP)
        part_a = jnp.einsum("rk,kri->ri", fc, part_y, precision=HP)
        part_c = jnp.einsum("kri,ri->rk", part_y, fa, precision=HP)
        part_b = jnp.einsum("rk,krj->rj", fc, part_z, precision=HP)
        to_row = jnp.stack([row_message(part_b, gram_a, part_c, q) for q in range(4)])
        to_col = jnp.stack([jnp.stack([col_message(part_a, gram_b, part_c, h, q) for q in range(4)]) for h in range(2)])
        sent = jnp.where(same, to_row[None], to_col).reshape(8, 24, 128)
        got = lax.all_to_all(sent, NEAR, 0, 0).reshape(2, 4, 24, 128)
        near = got.sum(1)
        mine = lax.dynamic_index_in_dim(near, x_lo, 0, False)
        other = lax.dynamic_index_in_dim(near, 1 - x_lo, 0, False)
        for_row = jnp.where(lanes_c, mine + other, mine)
        own = lax.dynamic_index_in_dim(to_col[:, 0], x_lo, 0, False)
        across = lax.dynamic_index_in_dim(got, 1 - x_lo, 0, False)
        for_col = own + lax.dynamic_index_in_dim(across, chip, 0, False)
        for_row = sum_over(for_row, "z", 8)
        for_col = sum_over(jnp.where(lanes_c, for_row, for_col), "y", 8)
        for_row = jnp.where(lanes_c, for_col, for_row)
        sent = jnp.where(same, for_row[None, None], for_col[None, None])
        sent = jnp.broadcast_to(sent, (2, 4, 24, 128)).reshape(8, 24, 128)
        got = lax.all_to_all(sent, NEAR, 0, 0).reshape(2, 4, 24, 128)
        mine = lax.dynamic_index_in_dim(got, x_lo, 0, False)
        across = lax.dynamic_index_in_dim(got, 1 - x_lo, 0, False)
        other = lax.dynamic_index_in_dim(across, chip, 0, False)
        low = jnp.where(x_lo == 0, for_col, other)
        high = jnp.where(x_lo == 0, other, for_col)
        mode_a = jnp.concatenate([low[:16], high[:16]], 0)
        gram_b = jnp.concatenate([low[16:, :32], low[16:, 32:64], high[16:, :32], high[16:, 32:64]], 0)
        mode_b = jnp.concatenate([mine[:, :8].reshape(32, 128), mine[:, 8:16].reshape(32, 128)], 1)
        gram_a = mine[:, 16:, :32].reshape(32, 32)
        mode_c = mine[:, 16:, 64:72].reshape(32, 8)
        next_a = descend(fa, gram_b * gram_c, mode_a)
        next_b = descend(fb, gram_a * gram_c, mode_b)
        next_c = descend(fc, gram_a * gram_b, mode_c)
        fa, fb, fc = (next_a, next_b, next_c)
    return (fa, fb, fc)


def solution(mesh):
    rows, cols = mesh.devices.shape
    devices = mesh.devices.reshape(2, rows // 4, 2, cols // 2, 2)
    fine = Mesh(devices, ("x_hi", "z", "core", "y", "x_lo"))
    row, col = (("x_hi", "z", "core"), ("y", "x_lo"))
    in_specs = (P(None, row, col), P(None, row), P(None, col), P())
    out_specs = (P(None, row), P(None, col), P())
    return jax.shard_map(shards, mesh=fine, in_specs=in_specs, out_specs=out_specs, check_vma=False)
```

```python
import functools

import jax
import jax.numpy as jnp
from jax import lax
from jax.experimental import pallas as pl
from jax.experimental.pallas import tpu as pltpu
from jax.sharding import Mesh, PartitionSpec as P

ITERS = 6

HP = lax.Precision.HIGHEST
F32, BF16 = (jnp.float32, jnp.bfloat16)
NEAR = ("x_lo", "x_hi", "core")
VMEM = pl.BlockSpec(memory_space=pltpu.VMEM)
SMEM = pl.BlockSpec(memory_space=pltpu.SMEM)


def product(a, b, contract=(1, 0), precision=HP):
    dims = (((contract[0],), (contract[1],)), ((), ()))
    return lax.dot_general(a, b, dims, precision=precision, preferred_element_type=F32)


def split(x):
    high = x.astype(BF16)
    return high, (x - high.astype(F32)).astype(BF16)


def inverse_norm(matrix):
    return 1.0 / jnp.sqrt(jnp.sum(matrix * matrix, keepdims=True) + 1e-06)


def descend(factor, hessian, contraction):
    return factor - inverse_norm(hessian) * (product(hessian, factor) - contraction)


def prepare(t_ref, wz_ref, wy_ref):
    for k in range(8):
        high, low = split(t_ref[k])
        wz_ref[:128, 256 * k : 256 * k + 256] = high
        wz_ref[128:, 256 * k : 256 * k + 256] = low
        high, low = split(t_ref[k].T)
        wy_ref[0, :, 128 * k : 128 * k + 128] = high
        wy_ref[1, :, 128 * k : 128 * k + 128] = low


def update(x_lo, chip, got_ref, col_ref, fa, fb, fc):
    mine = [got_ref[4 * x_lo + q] for q in range(4)]
    other = got_ref[4 * (1 - x_lo) + chip]
    low = jnp.where(x_lo == 0, col_ref[...], other)
    high = jnp.where(x_lo == 0, other, col_ref[...])
    mode_a = jnp.concatenate([low[:16], high[:16]], 0)
    gram_b = jnp.concatenate([low[16:, :32], low[16:, 32:64], high[16:, :32], high[16:, 32:64]], 0)
    mode_b = jnp.concatenate([jnp.concatenate([m[:8], m[8:16]], 1) for m in mine], 0)
    gram_a = jnp.concatenate([m[16:, :32] for m in mine], 0)
    mode_c = jnp.concatenate([m[16:, 64:72] for m in mine], 0)
    gram_c = product(fc, fc, (1, 1))
    next_a = descend(fa, gram_b * gram_c, mode_a)
    next_b = descend(fb, gram_a * gram_c, mode_b)
    next_c = descend(fc, gram_a * gram_b, mode_c)
    return next_a, next_b, next_c


def contract(x_lo, fa, fb, fc, wz_ref, wy_ref, sent_ref, own_ref):
    a_high, a_low = split(fa)
    b_high, b_low = split(fb)
    left = jnp.concatenate([jnp.concatenate([a_high, a_high], 1), jnp.concatenate([a_low, jnp.zeros_like(a_low)], 1)], 0)
    z = product(left, wz_ref[...], precision=None)
    z = z[:32] + z[32:]
    y = product(jnp.concatenate([b_high, b_low], 0), wy_ref[0], precision=None)
    y = y[:32] + y[32:] + product(b_high, wy_ref[1], precision=None)
    lane = lax.broadcasted_iota(jnp.int32, (32, 128), 1)
    part_a = jnp.zeros((32, 128), F32)
    part_b = jnp.zeros((32, 256), F32)
    part_c = jnp.zeros((32, 128), F32)
    for k in range(8):
        weight = fc[:, k : k + 1]
        y_k = y[:, 128 * k : 128 * k + 128]
        part_a += weight * y_k
        part_b += weight * z[:, 256 * k : 256 * k + 256]
        part_c = jnp.where(lane == 64 + k, jnp.sum(y_k * fa, 1, keepdims=True), part_c)
    gram_a = product(fa, jnp.concatenate([fa, jnp.zeros((96, 128), F32)], 0), (1, 1))
    gram_b = product(fb, jnp.concatenate([fb, jnp.zeros((96, 256), F32)], 0), (1, 1))
    row_tile = gram_a + part_c
    for q in range(4):
        rows = slice(8 * q, 8 * q + 8)
        at = 4 * x_lo + q
        sent_ref[at, 0:8] = part_b[rows, :128]
        sent_ref[at, 8:16] = part_b[rows, 128:]
        sent_ref[at, 16:24] = row_tile[rows]
    first = x_lo == 0
    tile_low = gram_b[:8] + pltpu.roll(gram_b[8:16], 32, 1)
    tile_high = gram_b[16:24] + pltpu.roll(gram_b[24:], 32, 1)
    own_ref[:16] = jnp.where(first, part_a[:16], part_a[16:])
    own_ref[16:] = jnp.where(first, tile_low, tile_high)
    across = jnp.where(first, part_a[16:], part_a[:16])
    tile = jnp.where(first, tile_high, tile_low)
    for q in range(4):
        at = 4 * (1 - x_lo) + q
        sent_ref[at, 0:16] = across
        sent_ref[at, 16:24] = tile + part_c[8 * q : 8 * q + 8]


def first_kernel(place_ref, fa_ref, fb_ref, fc_ref, wz_ref, wy_ref, sent_ref, own_ref):
    contract(place_ref[0], fa_ref[...], fb_ref[...], fc_ref[...], wz_ref, wy_ref, sent_ref, own_ref)


def middle_kernel(place_ref, got_ref, col_ref, fa_ref, fb_ref, fc_ref, wz_ref, wy_ref, na_ref, nb_ref, nc_ref, sent_ref, own_ref):
    x_lo = place_ref[0]
    fa, fb, fc = update(x_lo, place_ref[1], got_ref, col_ref, fa_ref[...], fb_ref[...], fc_ref[...])
    na_ref[...] = fa
    nb_ref[...] = fb
    nc_ref[...] = fc
    contract(x_lo, fa, fb, fc, wz_ref, wy_ref, sent_ref, own_ref)


def last_kernel(place_ref, got_ref, col_ref, fa_ref, fb_ref, fc_ref, na_ref, nb_ref, nc_ref):
    fa, fb, fc = update(place_ref[0], place_ref[1], got_ref, col_ref, fa_ref[...], fb_ref[...], fc_ref[...])
    na_ref[...] = fa
    nb_ref[...] = fb
    nc_ref[...] = fc


def call(kernel, outs, *args):
    shapes = [jax.ShapeDtypeStruct(s, d) for s, d in outs]
    specs = [SMEM if a.dtype == jnp.int32 else VMEM for a in args]
    params = pltpu.CompilerParams(vmem_limit_bytes=16 * 1024 * 1024)
    return pl.pallas_call(kernel, out_shape=shapes, in_specs=specs, out_specs=[VMEM] * len(shapes), compiler_params=params)(*args)


def sum_over(block, axis, size):
    copies = jnp.broadcast_to(block[None], (size,) + block.shape)
    return lax.all_to_all(copies, axis, 0, 0).sum(0)


FACTORS = [((32, 128), F32), ((32, 256), F32), ((32, 8), F32)]
MESSAGES = [((8, 24, 128), F32), ((24, 128), F32)]


def shards(size_z, size_y, tensor, factor_a, factor_b, factor_c):
    factors = (factor_a, factor_b, factor_c)
    x_lo = lax.axis_index("x_lo")
    chip = lax.axis_index("x_hi") * 2 + lax.axis_index("core")
    place = jnp.stack([x_lo, chip]).astype(jnp.int32)
    same = jnp.arange(2)[:, None, None, None] == x_lo
    lane = jnp.arange(128)[None, :]
    lanes_c = (jnp.arange(24)[:, None] >= 16) & (lane >= 64)
    weights = call(prepare, [((256, 2048), BF16), ((2, 256, 1024), BF16)], tensor)
    sent, own = call(first_kernel, MESSAGES, place, *factors, *weights)
    for step in range(ITERS):
        got = lax.all_to_all(sent, NEAR, 0, 0).reshape(2, 4, 24, 128)
        near = got.sum(1)
        mine = lax.dynamic_index_in_dim(near, x_lo, 0, False)
        other = lax.dynamic_index_in_dim(near, 1 - x_lo, 0, False)
        for_row = jnp.where(lanes_c, mine + other, mine)
        across = lax.dynamic_index_in_dim(got, 1 - x_lo, 0, False)
        for_col = own + lax.dynamic_index_in_dim(across, chip, 0, False)
        for_row = sum_over(for_row, "z", size_z)
        for_col = sum_over(jnp.where(lanes_c, for_row, for_col), "y", size_y)
        for_row = jnp.where(lanes_c, for_col, for_row)
        sent = jnp.where(same, for_row[None, None], for_col[None, None])
        sent = jnp.broadcast_to(sent, (2, 4, 24, 128)).reshape(8, 24, 128)
        got = lax.all_to_all(sent, NEAR, 0, 0)
        if step < ITERS - 1:
            *factors, sent, own = call(middle_kernel, FACTORS + MESSAGES, place, got, for_col, *factors, *weights)
        else:
            factors = call(last_kernel, FACTORS, place, got, for_col, *factors)
    return tuple(factors)


def solution(mesh):
    rows, cols = mesh.devices.shape
    devices = mesh.devices.reshape(2, rows // 4, 2, cols // 2, 2)
    fine = Mesh(devices, ("x_hi", "z", "core", "y", "x_lo"))
    row, col = (("x_hi", "z", "core"), ("y", "x_lo"))
    in_specs = (P(None, row, col), P(None, row), P(None, col), P())
    out_specs = (P(None, row), P(None, col), P())
    body = functools.partial(shards, rows // 4, cols // 2)
    return jax.shard_map(body, mesh=fine, in_specs=in_specs, out_specs=out_specs, check_vma=False)
```

```python
import functools

import jax
import jax.numpy as jnp
from jax import lax
from jax.experimental import pallas as pl
from jax.experimental.pallas import tpu as pltpu
from jax.sharding import Mesh, PartitionSpec as P

ITERS = 6

HP = lax.Precision.HIGHEST
F32, BF16 = (jnp.float32, jnp.bfloat16)
VMEM = pl.BlockSpec(memory_space=pltpu.VMEM)
SMEM = pl.BlockSpec(memory_space=pltpu.SMEM)


def product(a, b, contract=(1, 0), precision=HP):
    dims = (((contract[0],), (contract[1],)), ((), ()))
    return lax.dot_general(a, b, dims, precision=precision, preferred_element_type=F32)


def split(x):
    high = x.astype(BF16)
    return high, (x - high.astype(F32)).astype(BF16)


def inverse_norm(matrix):
    return 1.0 / jnp.sqrt(jnp.sum(matrix * matrix, keepdims=True) + 1e-06)


def descend(factor, hessian, contraction):
    return factor - inverse_norm(hessian) * (product(hessian, factor) - contraction)


def prepare(t_ref, wz_ref, wy_ref):
    for k in range(8):
        high, low = split(t_ref[k])
        wz_ref[:128, 256 * k : 256 * k + 256] = high
        wz_ref[128:, 256 * k : 256 * k + 256] = low
        high, low = split(t_ref[k].T)
        wy_ref[0, :, 128 * k : 128 * k + 128] = high
        wy_ref[1, :, 128 * k : 128 * k + 128] = low


def pack(square):
    tiles = [square[8 * q : 8 * q + 8] for q in range(4)]
    return tiles[0] + sum(pltpu.roll(tiles[q], 32 * q, 1) for q in range(1, 4))


def unpack(tile, width):
    return jnp.concatenate([tile[:, 32 * q : 32 * q + width] for q in range(4)], 0)


def widen(x):
    return jnp.concatenate([x, jnp.zeros((128 - x.shape[0], x.shape[1]), F32)], 0)


def update(core, both_ref, fa, fb, fc):
    rows, cols = (both_ref[0], both_ref[1])
    mode_a = jnp.where(core == 0, cols[:32], cols[32:64])
    mode_b = jnp.concatenate([rows[:32], rows[32:64]], 1)
    gram_a, gram_b = (unpack(rows[64:72], 32), unpack(cols[64:72], 32))
    gram_c = product(fc, fc, (1, 1))
    next_a = descend(fa, gram_b * gram_c, mode_a)
    next_b = descend(fb, gram_a * gram_c, mode_b)
    h_c = gram_a * gram_b
    scale = inverse_norm(h_c)
    return next_a, next_b, fc - scale * product(h_c, fc), scale


def add_mode_c(base, scale, ring_ref):
    total = ring_ref[0]
    for n in range(1, ring_ref.shape[0] // 2):
        total += ring_ref[2 * n]
    return base + scale * unpack(total, 8)


def multiply(fa, fb, wz_ref, wy_ref):
    a_high, a_low = split(fa)
    b_high, b_low = split(fb)
    left = jnp.concatenate([jnp.concatenate([a_high, a_high], 1), jnp.concatenate([a_low, jnp.zeros_like(a_low)], 1)], 0)
    z = product(left, wz_ref[...], precision=None)
    z = z[:32] + z[32:]
    y = product(jnp.concatenate([b_high, b_low], 0), wy_ref[0], precision=None)
    y = y[:32] + y[32:] + product(b_high, wy_ref[1], precision=None)
    lane = lax.broadcasted_iota(jnp.int32, (32, 128), 1)
    part_c = jnp.zeros((32, 128), F32)
    for k in range(8):
        part_c = jnp.where(lane == k, jnp.sum(y[:, 128 * k : 128 * k + 128] * fa, 1, keepdims=True), part_c)
    gram_a = product(fa, widen(fa), (1, 1))
    gram_b = product(fb, widen(fb), (1, 1))
    return y, z, pack(gram_a), pack(gram_b), pack(part_c)


def message(fc, y, z, gram_a, gram_b, part_c, sent_ref):
    part_a = jnp.zeros((32, 128), F32)
    part_b = jnp.zeros((32, 256), F32)
    for k in range(8):
        weight = fc[:, k : k + 1]
        part_a += weight * y[:, 128 * k : 128 * k + 128]
        part_b += weight * z[:, 256 * k : 256 * k + 256]
    for n in range(4):
        sent_ref[2 * n, 0:32] = part_b[:, :128]
        sent_ref[2 * n, 32:64] = part_b[:, 128:]
        sent_ref[2 * n, 64:72] = gram_a
        sent_ref[2 * n, 72:80] = part_c
        sent_ref[2 * n + 1, 0:32] = part_a
        sent_ref[2 * n + 1, 32:64] = jnp.zeros((32, 128), F32)
        sent_ref[2 * n + 1, 64:72] = gram_b
        sent_ref[2 * n + 1, 72:80] = part_c


def first_kernel(fa_ref, fb_ref, fc_ref, wz_ref, wy_ref, sent_ref):
    message(fc_ref[...], *multiply(fa_ref[...], fb_ref[...], wz_ref, wy_ref), sent_ref)


def near_kernel(place_ref, got_ref, out_ref):
    x_hi, x_lo, core = (place_ref[0], place_ref[1], place_ref[2])
    rows = [got_ref[4 * h + 2 * x_lo + c, 0:72] for h in range(2) for c in range(2)]
    rows = (rows[0] + rows[1]) + (rows[2] + rows[3])
    at = 4 * x_hi
    block_0 = got_ref[at, 0:32] + got_ref[at + 2, 0:32]
    block_1 = got_ref[at + 1, 0:32] + got_ref[at + 3, 0:32]
    gram_b = got_ref[at + 1, 64:72] + got_ref[at + 3, 64:72]
    cols = jnp.concatenate([block_0, block_1, gram_b], 0)
    part_c = got_ref[0, 72:80]
    for n in range(1, 8):
        part_c += got_ref[n, 72:80]
    out = jnp.where(core == 0, rows, cols)
    for n in range(out_ref.shape[0]):
        out_ref[n, 0:72] = out
        out_ref[n, 72:80] = part_c


def ring_kernel(got_ref, sum_ref, ring_ref):
    total = got_ref[0]
    for n in range(1, got_ref.shape[0]):
        total += got_ref[n]
    sum_ref[...] = total[:72]
    for n in range(ring_ref.shape[0]):
        ring_ref[n] = total[72:]


def factor_kernel(place_ref, both_ref, fa_ref, fb_ref, fc_ref, wz_ref, wy_ref, na_ref, nb_ref, base_ref, scale_ref, y_ref, z_ref, packs_ref):
    fa, fb, base, scale = update(place_ref[2], both_ref, fa_ref[...], fb_ref[...], fc_ref[...])
    na_ref[...] = fa
    nb_ref[...] = fb
    base_ref[...] = base
    scale_ref[...] = jnp.broadcast_to(scale, (8, 128))
    y, z, *packs = multiply(fa, fb, wz_ref, wy_ref)
    y_ref[...] = y
    z_ref[...] = z
    for n in range(3):
        packs_ref[n] = packs[n]


def send_kernel(ring_ref, base_ref, scale_ref, y_ref, z_ref, packs_ref, nc_ref, sent_ref):
    fc = add_mode_c(base_ref[...], scale_ref[:1, :1], ring_ref)
    nc_ref[...] = fc
    message(fc, y_ref[...], z_ref[...], packs_ref[0], packs_ref[1], packs_ref[2], sent_ref)


def last_kernel(place_ref, both_ref, ring_ref, fa_ref, fb_ref, fc_ref, na_ref, nb_ref, nc_ref):
    fa, fb, base, scale = update(place_ref[2], both_ref, fa_ref[...], fb_ref[...], fc_ref[...])
    na_ref[...] = fa
    nb_ref[...] = fb
    nc_ref[...] = add_mode_c(base, scale, ring_ref)


def call(kernel, outs, *args):
    shapes = [jax.ShapeDtypeStruct(s, d) for s, d in outs]
    specs = [SMEM if a.dtype == jnp.int32 else VMEM for a in args]
    params = pltpu.CompilerParams(vmem_limit_bytes=16 * 1024 * 1024)
    cost = pl.CostEstimate(flops=100_000_000, bytes_accessed=4_000_000, transcendentals=0)
    return pl.pallas_call(kernel, out_shape=shapes, in_specs=specs, out_specs=[VMEM] * len(shapes), compiler_params=params, cost_estimate=cost)(*args)


A, B, C = (((32, 128), F32), ((32, 256), F32), ((32, 8), F32))
SENT = ((8, 80, 128), F32)
PRODUCTS = [((8, 128), F32), ((32, 1024), F32), ((32, 2048), F32), ((3, 8, 128), F32)]
NEAR = ("x_hi", "x_lo", "core")
ALL = ("x_hi", "z", "core", "y", "x_lo")


def rings(size_z, size_y):
    def at(x_hi, z, core, y, x_lo):
        return (((x_hi * size_z + z) * 2 + core) * size_y + y) * 2 + x_lo

    pairs = [(x_hi, x_lo) for x_hi in range(2) for x_lo in range(2)]
    along_z = [[at(h, z, 0, y, l) for z in range(size_z)] for h, l in pairs for y in range(size_y)]
    along_y = [[at(h, z, 1, y, l) for y in range(size_y)] for h, l in pairs for z in range(size_z)]
    return along_z + along_y


def shards(size_z, size_y, tensor, factor_a, factor_b, factor_c):
    fa, fb, fc = (factor_a, factor_b, factor_c)
    place = jnp.stack([lax.axis_index(name) for name in NEAR]).astype(jnp.int32)
    groups = rings(size_z, size_y)
    weights = call(prepare, [((256, 2048), BF16), ((2, 256, 1024), BF16)], tensor)
    (sent,) = call(first_kernel, [SENT], fa, fb, fc, *weights)
    for step in range(ITERS):
        got = lax.all_to_all(sent, NEAR, 0, 0)
        (sent,) = call(near_kernel, [((size_z, 80, 128), F32)], place, got)
        got = lax.all_to_all(sent, ALL, 0, 0, axis_index_groups=groups)
        sums, ring = call(ring_kernel, [((72, 128), F32), ((2 * size_y, 8, 128), F32)], got)
        ring = lax.all_to_all(ring, ("y", "core"), 0, 0)
        both = lax.all_gather(sums, "core")
        if step < ITERS - 1:
            fa, fb, *rest = call(factor_kernel, [A, B, C] + PRODUCTS, place, both, fa, fb, fc, *weights)
            fc, sent = call(send_kernel, [C, SENT], ring, *rest)
        else:
            fa, fb, fc = call(last_kernel, [A, B, C], place, both, ring, fa, fb, fc)
    return (fa, fb, fc)


def solution(mesh):
    rows, cols = mesh.devices.shape
    devices = mesh.devices.reshape(2, rows // 4, 2, cols // 2, 2)
    fine = Mesh(devices, ("x_hi", "z", "core", "y", "x_lo"))
    row, col = (("x_hi", "z", "core"), ("y", "x_lo"))
    in_specs = (P(None, row, col), P(None, row), P(None, col), P())
    out_specs = (P(None, row), P(None, col), P())
    body = functools.partial(shards, rows // 4, cols // 2)
    return jax.shard_map(body, mesh=fine, in_specs=in_specs, out_specs=out_specs, check_vma=False)
```

```python
import functools

import jax
import jax.numpy as jnp
from jax import lax
from jax.experimental import pallas as pl
from jax.experimental.pallas import tpu as pltpu
from jax.sharding import Mesh, PartitionSpec as P

ITERS = 6

HP = lax.Precision.HIGHEST
F32, BF16 = (jnp.float32, jnp.bfloat16)
VMEM = pl.BlockSpec(memory_space=pltpu.VMEM)
SMEM = pl.BlockSpec(memory_space=pltpu.SMEM)


def product(a, b, contract=(1, 0), precision=HP):
    dims = (((contract[0],), (contract[1],)), ((), ()))
    return lax.dot_general(a, b, dims, precision=precision, preferred_element_type=F32)


def split(x):
    high = x.astype(BF16)
    return high, (x - high.astype(F32)).astype(BF16)


def inverse_norm(matrix):
    return 1.0 / jnp.sqrt(jnp.sum(matrix * matrix, keepdims=True) + 1e-06)


def descend(factor, hessian, contraction):
    return factor - inverse_norm(hessian) * (product(hessian, factor) - contraction)


def prepare(t_ref, wz_ref, wy_ref):
    for k in range(8):
        high, low = split(t_ref[k])
        wz_ref[:128, 256 * k : 256 * k + 256] = high
        wz_ref[128:, 256 * k : 256 * k + 256] = low
        high, low = split(t_ref[k].T)
        wy_ref[0, :, 128 * k : 128 * k + 128] = high
        wy_ref[1, :, 128 * k : 128 * k + 128] = low


def pack(square, first, step):
    tiles = [square[8 * q : 8 * q + 8] for q in range(4)]
    return sum(pltpu.roll(tiles[q], first + step * q, 1) if first + q else tiles[q] for q in range(4))


def widen(x):
    return jnp.concatenate([x, jnp.zeros((128 - x.shape[0], x.shape[1]), F32)], 0)


def unpack_gram(halves):
    return jnp.concatenate([half[32:40, 32 * q : 32 * q + 32] for half in halves for q in range(2)], 0)


def update(core, both_ref, fa, fb, fc):
    rows = [both_ref[0, h] for h in range(2)]
    cols = [both_ref[1, h] for h in range(2)]
    mode_a = jnp.concatenate([jnp.where(core == 0, col[:16], col[16:32]) for col in cols], 0)
    mode_b = jnp.concatenate([jnp.concatenate([row[:16], row[16:32]], 1) for row in rows], 0)
    gram_a, gram_b = (unpack_gram(rows), unpack_gram(cols))
    gram_c = product(fc, fc, (1, 1))
    next_a = descend(fa, gram_b * gram_c, mode_a)
    next_b = descend(fb, gram_a * gram_c, mode_b)
    h_c = gram_a * gram_b
    scale = inverse_norm(h_c)
    return next_a, next_b, fc - scale * product(h_c, fc), scale


def add_mode_c(base, scale, ring_ref):
    total = ring_ref[0]
    for n in range(1, ring_ref.shape[0] // 2):
        total += ring_ref[2 * n]
    mode_c = jnp.concatenate([total[:, 64 + 8 * q : 72 + 8 * q] for q in range(4)], 0)
    return base + scale * mode_c


def multiply(fa, fb, wz_ref, wy_ref):
    a_high, a_low = split(fa)
    b_high, b_low = split(fb)
    left = jnp.concatenate([jnp.concatenate([a_high, a_high], 1), jnp.concatenate([a_low, jnp.zeros_like(a_low)], 1)], 0)
    z = product(left, wz_ref[...], precision=None)
    z = z[:32] + z[32:]
    y = product(jnp.concatenate([b_high, b_low], 0), wy_ref[0], precision=None)
    y = y[:32] + y[32:] + product(b_high, wy_ref[1], precision=None)
    lane = lax.broadcasted_iota(jnp.int32, (32, 128), 1)
    part_c = jnp.zeros((32, 128), F32)
    for k in range(8):
        part_c = jnp.where(lane == k, jnp.sum(y[:, 128 * k : 128 * k + 128] * fa, 1, keepdims=True), part_c)
    gram_a = product(fa, widen(fa), (1, 1))
    gram_b = product(fb, widen(fb), (1, 1))
    return y, z, pack(gram_a, 0, 32), pack(gram_b, 0, 32), pack(part_c, 64, 8)


def message(fc, y, z, gram_a, part_c, sent_ref):
    part_a = jnp.zeros((32, 128), F32)
    part_b = jnp.zeros((32, 256), F32)
    for k in range(8):
        weight = fc[:, k : k + 1]
        part_a += weight * y[:, 128 * k : 128 * k + 128]
        part_b += weight * z[:, 256 * k : 256 * k + 256]
    sent_ref[0:32] = part_b[:, :128]
    sent_ref[32:64] = part_b[:, 128:]
    sent_ref[64:96] = part_a
    sent_ref[96:104] = gram_a
    sent_ref[104:112] = part_c


def first_kernel(fa_ref, fb_ref, fc_ref, wz_ref, wy_ref, gram_ref, sent_ref):
    y, z, gram_a, gram_b, part_c = multiply(fa_ref[...], fb_ref[...], wz_ref, wy_ref)
    gram_ref[...] = gram_b
    message(fc_ref[...], y, z, gram_a, part_c, sent_ref)


def chip_kernel(place_ref, both_ref, gram_ref, out_ref):
    first = place_ref[0] == 0
    low = jnp.where(first, both_ref[0, 0:32] + both_ref[1, 0:32], both_ref[0, 64:96])
    high = jnp.where(first, both_ref[0, 32:64] + both_ref[1, 32:64], both_ref[1, 64:96])
    gram = jnp.where(first, both_ref[0, 96:104] + both_ref[1, 96:104], gram_ref[...])
    part_c = both_ref[0, 104:112] + both_ref[1, 104:112]
    lane = lax.broadcasted_iota(jnp.int32, (8, 128), 1)
    ring = out_ref.shape[0] // 2
    for h in range(2):
        tile = jnp.where(lane < 64, pltpu.roll(gram, 64, 1) if h else gram, part_c)
        for n in range(h * ring, h * ring + ring):
            out_ref[n, 0:16] = low[16 * h : 16 * h + 16]
            out_ref[n, 16:32] = high[16 * h : 16 * h + 16]
            out_ref[n, 32:40] = tile


def ring_kernel(got_ref, sum_ref, ring_ref):
    total = got_ref[0]
    for n in range(1, got_ref.shape[0]):
        total += got_ref[n]
    sum_ref[...] = total
    for n in range(ring_ref.shape[0]):
        ring_ref[n] = total[32:]


def factor_kernel(place_ref, both_ref, fa_ref, fb_ref, fc_ref, wz_ref, wy_ref, na_ref, nb_ref, gram_ref, base_ref, scale_ref, y_ref, z_ref, packs_ref):
    fa, fb, base, scale = update(place_ref[0], both_ref, fa_ref[...], fb_ref[...], fc_ref[...])
    na_ref[...] = fa
    nb_ref[...] = fb
    base_ref[...] = base
    scale_ref[...] = jnp.broadcast_to(scale, (8, 128))
    y, z, gram_a, gram_b, part_c = multiply(fa, fb, wz_ref, wy_ref)
    y_ref[...] = y
    z_ref[...] = z
    gram_ref[...] = gram_b
    packs_ref[0] = gram_a
    packs_ref[1] = part_c


def send_kernel(ring_ref, base_ref, scale_ref, y_ref, z_ref, packs_ref, nc_ref, sent_ref):
    fc = add_mode_c(base_ref[...], scale_ref[:1, :1], ring_ref)
    nc_ref[...] = fc
    message(fc, y_ref[...], z_ref[...], packs_ref[0], packs_ref[1], sent_ref)


def last_kernel(place_ref, both_ref, ring_ref, fa_ref, fb_ref, fc_ref, na_ref, nb_ref, nc_ref):
    fa, fb, base, scale = update(place_ref[0], both_ref, fa_ref[...], fb_ref[...], fc_ref[...])
    na_ref[...] = fa
    nb_ref[...] = fb
    nc_ref[...] = add_mode_c(base, scale, ring_ref)


def call(kernel, outs, *args):
    shapes = [jax.ShapeDtypeStruct(s, d) for s, d in outs]
    specs = [SMEM if a.dtype == jnp.int32 else VMEM for a in args]
    params = pltpu.CompilerParams(vmem_limit_bytes=16 * 1024 * 1024)
    cost = pl.CostEstimate(flops=100_000_000, bytes_accessed=4_000_000, transcendentals=0)
    return pl.pallas_call(kernel, out_shape=shapes, in_specs=specs, out_specs=[VMEM] * len(shapes), compiler_params=params, cost_estimate=cost)(*args)


A, B, C = (((32, 128), F32), ((32, 256), F32), ((32, 8), F32))
TILE, SENT = (((8, 128), F32), ((112, 128), F32))
PRODUCTS = [TILE, ((32, 1024), F32), ((32, 2048), F32), ((2, 8, 128), F32)]
ALL = ("x_hi", "z", "core", "y", "x_lo")


def groups_of(size_z, size_y):
    def at(x_hi, z, core, y, x_lo):
        return (((x_hi * size_z + z) * 2 + core) * size_y + y) * 2 + x_lo

    two, zs, ys = (range(2), range(size_z), range(size_y))
    rings = [[at(h, z, 0, y, l) for h in two for z in zs] for l in two for y in ys]
    rings += [[at(h, z, 1, y, l) for l in two for y in ys] for h in two for z in zs]
    pairs = [[at(h, z, 0, y, l) for h in two] for z in zs for y in ys for l in two]
    pairs += [[at(h, z, 1, y, l) for l in two] for z in zs for y in ys for h in two]
    return rings, pairs


def shards(size_z, size_y, tensor, factor_a, factor_b, factor_c):
    fa, fb, fc = (factor_a, factor_b, factor_c)
    place = lax.axis_index("core").reshape(1).astype(jnp.int32)
    rings, pairs = groups_of(size_z, size_y)
    weights = call(prepare, [((256, 2048), BF16), ((2, 256, 1024), BF16)], tensor)
    gram_b, sent = call(first_kernel, [TILE, SENT], fa, fb, fc, *weights)
    for step in range(ITERS):
        both = lax.all_gather(sent, "core")
        (sent,) = call(chip_kernel, [((2 * size_z, 40, 128), F32)], place, both, gram_b)
        got = lax.all_to_all(sent, ALL, 0, 0, axis_index_groups=rings)
        sums, ring = call(ring_kernel, [((40, 128), F32), ((4 * size_y, 8, 128), F32)], got)
        ring = lax.all_to_all(ring, ("y", "x_lo", "core"), 0, 0)
        both = lax.all_gather(sums, ALL, axis_index_groups=pairs)
        both = lax.all_gather(both, "core")
        if step < ITERS - 1:
            fa, fb, gram_b, *rest = call(factor_kernel, [A, B, TILE, C] + PRODUCTS, place, both, fa, fb, fc, *weights)
            fc, sent = call(send_kernel, [C, SENT], ring, *rest)
        else:
            fa, fb, fc = call(last_kernel, [A, B, C], place, both, ring, fa, fb, fc)
    return (fa, fb, fc)


def solution(mesh):
    rows, cols = mesh.devices.shape
    devices = mesh.devices.reshape(2, rows // 4, 2, cols // 2, 2)
    fine = Mesh(devices, ("x_hi", "z", "core", "y", "x_lo"))
    row, col = (("x_hi", "z", "core"), ("y", "x_lo"))
    in_specs = (P(None, row, col), P(None, row), P(None, col), P())
    out_specs = (P(None, row), P(None, col), P())
    body = functools.partial(shards, rows // 4, cols // 2)
    return jax.shard_map(body, mesh=fine, in_specs=in_specs, out_specs=out_specs, check_vma=False)
```

```python
import functools

import jax
import jax.numpy as jnp
from jax import lax
from jax.experimental import pallas as pl
from jax.experimental.pallas import tpu as pltpu
from jax.sharding import Mesh, PartitionSpec as P

ITERS = 6

HP = lax.Precision.HIGHEST
F32, BF16 = (jnp.float32, jnp.bfloat16)
VMEM = pl.BlockSpec(memory_space=pltpu.VMEM)
SMEM = pl.BlockSpec(memory_space=pltpu.SMEM)


def product(a, b, contract=(1, 0), precision=HP):
    dims = (((contract[0],), (contract[1],)), ((), ()))
    return lax.dot_general(a, b, dims, precision=precision, preferred_element_type=F32)


def split(x):
    high = x.astype(BF16)
    return high, (x - high.astype(F32)).astype(BF16)


def inverse_norm(matrix):
    return 1.0 / jnp.sqrt(jnp.sum(matrix * matrix, keepdims=True) + 1e-06)


def descend(factor, hessian, contraction):
    return factor - inverse_norm(hessian) * (product(hessian, factor) - contraction)


def prepare(t_ref, wz_ref, wy_ref):
    for k in range(8):
        high, low = split(t_ref[k])
        wz_ref[:128, 256 * k : 256 * k + 256] = high
        wz_ref[128:, 256 * k : 256 * k + 256] = low
        high, low = split(t_ref[k].T)
        wy_ref[0, :, 128 * k : 128 * k + 128] = high
        wy_ref[1, :, 128 * k : 128 * k + 128] = low


def pack(square, first, step):
    tiles = [square[8 * q : 8 * q + 8] for q in range(4)]
    return sum(pltpu.roll(tiles[q], first + step * q, 1) if first + q else tiles[q] for q in range(4))


def widen(x):
    return jnp.concatenate([x, jnp.zeros((128 - x.shape[0], x.shape[1]), F32)], 0)


def unpack_gram(halves):
    return jnp.concatenate([half[32:40, 32 * q : 32 * q + 32] for half in halves for q in range(2)], 0)


def update(core, both_ref, fa, fb, fc):
    rows = [both_ref[0, h] for h in range(2)]
    cols = [both_ref[1, h] for h in range(2)]
    mode_a = jnp.concatenate([jnp.where(core == 0, col[:16], col[16:32]) for col in cols], 0)
    mode_b = jnp.concatenate([jnp.concatenate([row[:16], row[16:32]], 1) for row in rows], 0)
    gram_a, gram_b = (unpack_gram(rows), unpack_gram(cols))
    gram_c = product(fc, fc, (1, 1))
    next_a = descend(fa, gram_b * gram_c, mode_a)
    next_b = descend(fb, gram_a * gram_c, mode_b)
    h_c = gram_a * gram_b
    scale = inverse_norm(h_c)
    return next_a, next_b, fc - scale * product(h_c, fc), scale


def add_mode_c(base, scale, ring_ref):
    total = ring_ref[0]
    for n in range(1, ring_ref.shape[0] // 2):
        total += ring_ref[n]
    mode_c = jnp.concatenate([total[:, 64 + 8 * q : 72 + 8 * q] for q in range(4)], 0)
    return base + scale * mode_c


def multiply(fa, fb, wz_ref, wy_ref):
    a_high, a_low = split(fa)
    b_high, b_low = split(fb)
    left = jnp.concatenate([jnp.concatenate([a_high, a_high], 1), jnp.concatenate([a_low, jnp.zeros_like(a_low)], 1)], 0)
    z = product(left, wz_ref[...], precision=None)
    z = z[:32] + z[32:]
    y = product(jnp.concatenate([b_high, b_low], 0), wy_ref[0], precision=None)
    y = y[:32] + y[32:] + product(b_high, wy_ref[1], precision=None)
    lane = lax.broadcasted_iota(jnp.int32, (32, 128), 1)
    part_c = jnp.zeros((32, 128), F32)
    for k in range(8):
        part_c = jnp.where(lane == k, jnp.sum(y[:, 128 * k : 128 * k + 128] * fa, 1, keepdims=True), part_c)
    gram_a = product(fa, widen(fa), (1, 1))
    gram_b = product(fb, widen(fb), (1, 1))
    return y, z, pack(gram_a, 0, 32), pack(gram_b, 0, 32), pack(part_c, 64, 8)


def message(fc, y, z, gram_a, part_c, sent_ref):
    part_a = jnp.zeros((32, 128), F32)
    part_b = jnp.zeros((32, 256), F32)
    for k in range(8):
        weight = fc[:, k : k + 1]
        part_a += weight * y[:, 128 * k : 128 * k + 128]
        part_b += weight * z[:, 256 * k : 256 * k + 256]
    sent_ref[0:32] = part_b[:, :128]
    sent_ref[32:64] = part_b[:, 128:]
    sent_ref[64:96] = part_a
    sent_ref[96:104] = gram_a
    sent_ref[104:112] = part_c


def first_kernel(fa_ref, fb_ref, fc_ref, wz_ref, wy_ref, gram_ref, sent_ref):
    y, z, gram_a, gram_b, part_c = multiply(fa_ref[...], fb_ref[...], wz_ref, wy_ref)
    gram_ref[...] = gram_b
    message(fc_ref[...], y, z, gram_a, part_c, sent_ref)


def chip_kernel(place_ref, both_ref, gram_ref, out_ref):
    first = place_ref[0] == 0
    low = jnp.where(first, both_ref[0, 0:32] + both_ref[1, 0:32], both_ref[0, 64:96])
    high = jnp.where(first, both_ref[0, 32:64] + both_ref[1, 32:64], both_ref[1, 64:96])
    gram = jnp.where(first, both_ref[0, 96:104] + both_ref[1, 96:104], gram_ref[...])
    part_c = both_ref[0, 104:112] + both_ref[1, 104:112]
    lane = lax.broadcasted_iota(jnp.int32, (8, 128), 1)
    for h in range(2):
        tile = jnp.where(lane < 64, pltpu.roll(gram, 64, 1) if h else gram, part_c)
        for n in range(h, out_ref.shape[0], 2):
            out_ref[n, 0:16] = low[16 * h : 16 * h + 16]
            out_ref[n, 16:32] = high[16 * h : 16 * h + 16]
            out_ref[n, 32:40] = tile


def ring_kernel(got_ref, sum_ref, ring_ref):
    total = got_ref[0]
    for n in range(1, got_ref.shape[0]):
        total += got_ref[n]
    sum_ref[...] = total
    for n in range(ring_ref.shape[0]):
        ring_ref[n] = total[32:]


def factor_kernel(place_ref, both_ref, fa_ref, fb_ref, fc_ref, wz_ref, wy_ref, na_ref, nb_ref, gram_ref, base_ref, scale_ref, y_ref, z_ref, packs_ref):
    fa, fb, base, scale = update(place_ref[0], both_ref, fa_ref[...], fb_ref[...], fc_ref[...])
    na_ref[...] = fa
    nb_ref[...] = fb
    base_ref[...] = base
    scale_ref[...] = jnp.broadcast_to(scale, (8, 128))
    y, z, gram_a, gram_b, part_c = multiply(fa, fb, wz_ref, wy_ref)
    y_ref[...] = y
    z_ref[...] = z
    gram_ref[...] = gram_b
    packs_ref[0] = gram_a
    packs_ref[1] = part_c


def send_kernel(ring_ref, base_ref, scale_ref, y_ref, z_ref, packs_ref, nc_ref, sent_ref):
    fc = add_mode_c(base_ref[...], scale_ref[:1, :1], ring_ref)
    nc_ref[...] = fc
    message(fc, y_ref[...], z_ref[...], packs_ref[0], packs_ref[1], sent_ref)


def last_kernel(place_ref, both_ref, ring_ref, fa_ref, fb_ref, fc_ref, na_ref, nb_ref, nc_ref):
    fa, fb, base, scale = update(place_ref[0], both_ref, fa_ref[...], fb_ref[...], fc_ref[...])
    na_ref[...] = fa
    nb_ref[...] = fb
    nc_ref[...] = add_mode_c(base, scale, ring_ref)


def call(kernel, outs, *args):
    shapes = [jax.ShapeDtypeStruct(s, d) for s, d in outs]
    specs = [SMEM if a.dtype == jnp.int32 else VMEM for a in args]
    params = pltpu.CompilerParams(vmem_limit_bytes=16 * 1024 * 1024)
    cost = pl.CostEstimate(flops=100_000_000, bytes_accessed=4_000_000, transcendentals=0)
    return pl.pallas_call(kernel, out_shape=shapes, in_specs=specs, out_specs=[VMEM] * len(shapes), compiler_params=params, cost_estimate=cost)(*args)


A, B, C = (((32, 128), F32), ((32, 256), F32), ((32, 8), F32))
TILE, SENT = (((8, 128), F32), ((112, 128), F32))
PRODUCTS = [TILE, ((32, 1024), F32), ((32, 2048), F32), ((2, 8, 128), F32)]
ALL = ("x_hi", "z", "core", "y", "x_lo")


def groups_of(size_z, size_y):
    def at(x_hi, z, core, y, x_lo):
        return (((x_hi * size_z + z) * 2 + core) * size_y + y) * 2 + x_lo

    two, zs, ys = (range(2), range(size_z), range(size_y))
    rings = [[at(h, z, 0, y, l) for h in two for z in zs] for l in two for y in ys]
    rings += [[at(h, z, 1, y, l) for y in ys for l in two] for h in two for z in zs]
    pairs = [[at(h, z, 0, y, l), at(h, z + 1, 0, y, l)] for h in two for z in zs[::2] for y in ys for l in two]
    pairs += [[at(h, z, 1, y, l) for l in two] for z in zs for y in ys for h in two]
    return rings, pairs


def shards(size_z, size_y, tensor, factor_a, factor_b, factor_c):
    fa, fb, fc = (factor_a, factor_b, factor_c)
    place = lax.axis_index("core").reshape(1).astype(jnp.int32)
    rings, pairs = groups_of(size_z, size_y)
    weights = call(prepare, [((256, 2048), BF16), ((2, 256, 1024), BF16)], tensor)
    gram_b, sent = call(first_kernel, [TILE, SENT], fa, fb, fc, *weights)
    for step in range(ITERS):
        both = lax.all_gather(sent, "core")
        (sent,) = call(chip_kernel, [((2 * size_z, 40, 128), F32)], place, both, gram_b)
        got = lax.all_to_all(sent, ALL, 0, 0, axis_index_groups=rings)
        sums, ring = call(ring_kernel, [((40, 128), F32), ((4 * size_y, 8, 128), F32)], got)
        ring = lax.all_to_all(ring, ("core", "y", "x_lo"), 0, 0)
        both = lax.all_gather(sums, ALL, axis_index_groups=pairs)
        both = lax.all_gather(both, "core")
        if step < ITERS - 1:
            fa, fb, gram_b, *rest = call(factor_kernel, [A, B, TILE, C] + PRODUCTS, place, both, fa, fb, fc, *weights)
            fc, sent = call(send_kernel, [C, SENT], ring, *rest)
        else:
            fa, fb, fc = call(last_kernel, [A, B, C], place, both, ring, fa, fb, fc)
    return (fa, fb, fc)


def solution(mesh):
    rows, cols = mesh.devices.shape
    devices = mesh.devices.reshape(2, rows // 4, 2, cols // 2, 2)
    fine = Mesh(devices, ("x_hi", "z", "core", "y", "x_lo"))
    row, col = (("x_hi", "z", "core"), ("y", "x_lo"))
    in_specs = (P(None, row, col), P(None, row), P(None, col), P())
    out_specs = (P(None, row), P(None, col), P())
    body = functools.partial(shards, rows // 4, cols // 2)
    return jax.shard_map(body, mesh=fine, in_specs=in_specs, out_specs=out_specs, check_vma=False)
```

```python
import functools

import jax
import jax.numpy as jnp
from jax import lax
from jax.experimental import pallas as pl
from jax.experimental.pallas import tpu as pltpu
from jax.sharding import Mesh, PartitionSpec as P

ITERS = 6

HP = lax.Precision.HIGHEST
F32, BF16 = (jnp.float32, jnp.bfloat16)
VMEM = pl.BlockSpec(memory_space=pltpu.VMEM)
SMEM = pl.BlockSpec(memory_space=pltpu.SMEM)


def product(a, b, contract=(1, 0), precision=HP):
    dims = (((contract[0],), (contract[1],)), ((), ()))
    return lax.dot_general(a, b, dims, precision=precision, preferred_element_type=F32)


def split(x):
    high = x.astype(BF16)
    return high, (x - high.astype(F32)).astype(BF16)


def inverse_norm(matrix):
    return 1.0 / jnp.sqrt(jnp.sum(matrix * matrix, keepdims=True) + 1e-06)


def descend(factor, hessian, contraction):
    return factor - inverse_norm(hessian) * (product(hessian, factor) - contraction)


def prepare(t_ref, wz_ref, wy_ref):
    for k in range(8):
        high, low = split(t_ref[k])
        wz_ref[:128, 256 * k : 256 * k + 256] = high
        wz_ref[128:, 256 * k : 256 * k + 256] = low
        high, low = split(t_ref[k].T)
        wy_ref[0, :, 128 * k : 128 * k + 128] = high
        wy_ref[1, :, 128 * k : 128 * k + 128] = low


def pack(square, first, step):
    tiles = [square[8 * q : 8 * q + 8] for q in range(4)]
    return sum(pltpu.roll(tiles[q], first + step * q, 1) if first + q else tiles[q] for q in range(4))


def widen(x):
    return jnp.concatenate([x, jnp.zeros((128 - x.shape[0], x.shape[1]), F32)], 0)


def unpack_gram(halves):
    return jnp.concatenate([half[32:40, 32 * q : 32 * q + 32] for half in halves for q in range(2)], 0)


def update(core, both_ref, fa, fb, fc):
    rows = [both_ref[0, h] for h in range(2)]
    cols = [both_ref[1, h] for h in range(2)]
    mode_a = jnp.concatenate([jnp.where(core == 0, col[:16], col[16:32]) for col in cols], 0)
    mode_b = jnp.concatenate([jnp.concatenate([row[:16], row[16:32]], 1) for row in rows], 0)
    gram_a, gram_b = (unpack_gram(rows), unpack_gram(cols))
    gram_c = product(fc, fc, (1, 1))
    next_a = descend(fa, gram_b * gram_c, mode_a)
    next_b = descend(fb, gram_a * gram_c, mode_b)
    h_c = gram_a * gram_b
    scale = inverse_norm(h_c)
    return next_a, next_b, fc - scale * product(h_c, fc), scale


def add_mode_c(base, scale, ring_ref):
    total = ring_ref[0]
    for n in range(1, ring_ref.shape[0] // 2):
        total += ring_ref[n]
    mode_c = jnp.concatenate([total[:, 64 + 8 * q : 72 + 8 * q] for q in range(4)], 0)
    return base + scale * mode_c


def multiply(fa, fb, wz_ref, wy_ref):
    a_high, a_low = split(fa)
    b_high, b_low = split(fb)
    left = jnp.concatenate([jnp.concatenate([a_high, a_high], 1), jnp.concatenate([a_low, jnp.zeros_like(a_low)], 1)], 0)
    z = product(left, wz_ref[...], precision=None)
    z = z[:32] + z[32:]
    y = product(jnp.concatenate([b_high, b_low], 0), wy_ref[0], precision=None)
    y = y[:32] + y[32:] + product(b_high, wy_ref[1], precision=None)
    lane = lax.broadcasted_iota(jnp.int32, (32, 128), 1)
    part_c = jnp.zeros((32, 128), F32)
    for k in range(8):
        part_c = jnp.where(lane == k, jnp.sum(y[:, 128 * k : 128 * k + 128] * fa, 1, keepdims=True), part_c)
    gram_a = product(fa, widen(fa), (1, 1))
    gram_b = product(fb, widen(fb), (1, 1))
    return y, z, pack(gram_a, 0, 32), pack(gram_b, 0, 32), pack(part_c, 64, 8)


def columns(wide):
    square = (lax.broadcasted_iota(jnp.int32, (8, 8), 0) == lax.broadcasted_iota(jnp.int32, (8, 8), 1)).astype(F32)
    return product(wide, square, (0, 0))


def keep_or_send(core, products, keep_ref, send_ref, gram_ref):
    y, z, gram_a, gram_b, part_c = products
    for block in range(16):
        rows = slice(32 * block, 32 * block + 32)
        z_block = z[:, 128 * block : 128 * block + 128]
        y_block = y[:, 128 * (block % 8) : 128 * (block % 8) + 128]
        keep_ref[rows] = jnp.where(core == 0, z_block, y_block)
        send_ref[rows] = jnp.where(core == 0, y_block, z_block)
    send_ref[512:520] = gram_a
    send_ref[520:528] = part_c
    gram_ref[...] = gram_b


def message(core, fc, both_ref, keep_ref, gram_ref, out_ref):
    def write(low, high, gram):
        part_c = both_ref[0, 520:528] + both_ref[1, 520:528]
        lane = lax.broadcasted_iota(jnp.int32, (8, 128), 1)
        for h in range(2):
            tile = jnp.where(lane < 64, pltpu.roll(gram, 64, 1) if h else gram, part_c)
            for n in range(h, out_ref.shape[0], 2):
                out_ref[n, 0:16] = low[16 * h : 16 * h + 16]
                out_ref[n, 16:32] = high[16 * h : 16 * h + 16]
                out_ref[n, 32:40] = tile

    @pl.when(core == 0)
    def _():
        low, high = (jnp.zeros((32, 128), F32), jnp.zeros((32, 128), F32))
        for k in range(8):
            weight = fc[:, k : k + 1]
            low += weight * (keep_ref[64 * k : 64 * k + 32] + both_ref[1, 64 * k : 64 * k + 32])
            high += weight * (keep_ref[64 * k + 32 : 64 * k + 64] + both_ref[1, 64 * k + 32 : 64 * k + 64])
        write(low, high, both_ref[0, 512:520] + both_ref[1, 512:520])

    @pl.when(core == 1)
    def _():
        low, high = (jnp.zeros((32, 128), F32), jnp.zeros((32, 128), F32))
        for k in range(8):
            weight = fc[:, k : k + 1]
            low += weight * both_ref[0, 32 * k : 32 * k + 32]
            high += weight * keep_ref[32 * k : 32 * k + 32]
        write(low, high, gram_ref[...])


def start_kernel(place_ref, t_ref, fa_ref, fb_ref, wz_ref, wy_ref, keep_ref, send_ref, gram_ref):
    prepare(t_ref, wz_ref, wy_ref)
    keep_or_send(place_ref[0], multiply(fa_ref[...], fb_ref[...], wz_ref, wy_ref), keep_ref, send_ref, gram_ref)


def first_kernel(place_ref, fc_ref, both_ref, keep_ref, gram_ref, nc_ref, out_ref):
    fc = columns(fc_ref[...])
    nc_ref[...] = fc
    message(place_ref[0], fc, both_ref, keep_ref, gram_ref, out_ref)


def ring_kernel(got_ref, sum_ref, ring_ref):
    total = got_ref[0]
    for n in range(1, got_ref.shape[0]):
        total += got_ref[n]
    sum_ref[...] = total
    for n in range(ring_ref.shape[0]):
        ring_ref[n] = total[32:]


def factor_kernel(place_ref, both_ref, fa_ref, fb_ref, fc_ref, wz_ref, wy_ref, na_ref, nb_ref, base_ref, scale_ref, keep_ref, send_ref, gram_ref):
    core = place_ref[0]
    fa, fb, base, scale = update(core, both_ref, fa_ref[...], fb_ref[...], fc_ref[...])
    na_ref[...] = fa
    nb_ref[...] = fb
    base_ref[...] = base
    scale_ref[...] = jnp.broadcast_to(scale, (8, 128))
    keep_or_send(core, multiply(fa, fb, wz_ref, wy_ref), keep_ref, send_ref, gram_ref)


def chip_kernel(place_ref, ring_ref, base_ref, scale_ref, both_ref, keep_ref, gram_ref, nc_ref, out_ref):
    fc = add_mode_c(base_ref[...], scale_ref[:1, :1], ring_ref)
    nc_ref[...] = fc
    message(place_ref[0], fc, both_ref, keep_ref, gram_ref, out_ref)


def last_kernel(place_ref, both_ref, ring_ref, fa_ref, fb_ref, fc_ref, na_ref, nb_ref, nc_ref):
    fa, fb, base, scale = update(place_ref[0], both_ref, fa_ref[...], fb_ref[...], fc_ref[...])
    na_ref[...] = fa
    nb_ref[...] = fb
    nc_ref[...] = add_mode_c(base, scale, ring_ref).T


def call(kernel, outs, *args):
    shapes = [jax.ShapeDtypeStruct(s, d) for s, d in outs]
    specs = [SMEM if a.dtype == jnp.int32 else VMEM for a in args]
    params = pltpu.CompilerParams(vmem_limit_bytes=16 * 1024 * 1024)
    cost = pl.CostEstimate(flops=100_000_000, bytes_accessed=4_000_000, transcendentals=0)
    return pl.pallas_call(kernel, out_shape=shapes, in_specs=specs, out_specs=[VMEM] * len(shapes), compiler_params=params, cost_estimate=cost)(*args)


A, B, C = (((32, 128), F32), ((32, 256), F32), ((32, 8), F32))
TILE = ((8, 128), F32)
PRODUCTS = [((512, 128), F32), ((528, 128), F32), TILE]
ALL = ("x_hi", "z", "core", "y", "x_lo")


def groups_of(size_z, size_y):
    def at(x_hi, z, core, y, x_lo):
        return (((x_hi * size_z + z) * 2 + core) * size_y + y) * 2 + x_lo

    two, zs, ys = (range(2), range(size_z), range(size_y))
    rings = [[at(h, z, 0, y, l) for h in two for z in zs] for l in two for y in ys]
    rings += [[at(h, z, 1, y, l) for y in ys for l in two] for h in two for z in zs]
    pairs = [[at(h, z, 0, y, l), at(h, z + 1, 0, y, l)] for h in two for z in zs[::2] for y in ys for l in two]
    pairs += [[at(h, z, 1, y, l) for l in two] for z in zs for y in ys for h in two]
    return rings, pairs


def shards(size_z, size_y, tensor, factor_a, factor_b, factor_c):
    fa, fb, fc = (factor_a, factor_b, factor_c)
    place = lax.axis_index("core").reshape(1).astype(jnp.int32)
    rings, pairs = groups_of(size_z, size_y)
    out = ((2 * size_z, 40, 128), F32)
    weights = [((256, 2048), BF16), ((2, 256, 1024), BF16)]
    *weights, keep, send, gram_b = call(start_kernel, weights + PRODUCTS, place, tensor, fa, fb)
    both = lax.all_gather(send, "core")
    fc, sent = call(first_kernel, [C, out], place, fc.T, both, keep, gram_b)
    for step in range(ITERS):
        got = lax.all_to_all(sent, ALL, 0, 0, axis_index_groups=rings)
        sums, ring = call(ring_kernel, [((40, 128), F32), ((4 * size_y, 8, 128), F32)], got)
        ring = lax.all_to_all(ring, ("core", "y", "x_lo"), 0, 0)
        both = lax.all_gather(sums, ALL, axis_index_groups=pairs)
        both = lax.all_gather(both, "core")
        if step < ITERS - 1:
            fa, fb, base, scale, keep, send, gram_b = call(factor_kernel, [A, B, C, TILE] + PRODUCTS, place, both, fa, fb, fc, *weights)
            both = lax.all_gather(send, "core")
            fc, sent = call(chip_kernel, [C, out], place, ring, base, scale, both, keep, gram_b)
        else:
            fa, fb, fc = call(last_kernel, [A, B, ((8, 32), F32)], place, both, ring, fa, fb, fc)
    return (fa, fb, fc.T)


def solution(mesh):
    rows, cols = mesh.devices.shape
    devices = mesh.devices.reshape(2, rows // 4, 2, cols // 2, 2)
    fine = Mesh(devices, ("x_hi", "z", "core", "y", "x_lo"))
    row, col = (("x_hi", "z", "core"), ("y", "x_lo"))
    in_specs = (P(None, row, col), P(None, row), P(None, col), P())
    out_specs = (P(None, row), P(None, col), P())
    body = functools.partial(shards, rows // 4, cols // 2)
    return jax.shard_map(body, mesh=fine, in_specs=in_specs, out_specs=out_specs, check_vma=False)
```

```python
import functools

import jax
import jax.numpy as jnp
from jax import lax
from jax.experimental import pallas as pl
from jax.experimental.pallas import tpu as pltpu
from jax.sharding import Mesh, PartitionSpec as P

ITERS = 6

HP = lax.Precision.HIGHEST
F32, BF16 = (jnp.float32, jnp.bfloat16)
VMEM = pl.BlockSpec(memory_space=pltpu.VMEM)
SMEM = pl.BlockSpec(memory_space=pltpu.SMEM)


def product(a, b, contract=(1, 0), precision=HP):
    dims = (((contract[0],), (contract[1],)), ((), ()))
    return lax.dot_general(a, b, dims, precision=precision, preferred_element_type=F32)


def split(x):
    high = x.astype(BF16)
    return high, (x - high.astype(F32)).astype(BF16)


def inverse_norm(matrix):
    return 1.0 / jnp.sqrt(jnp.sum(matrix * matrix, keepdims=True) + 1e-06)


def descend(factor, hessian, contraction):
    return factor - inverse_norm(hessian) * (product(hessian, factor) - contraction)


def prepare(t_ref, wz_ref, wy_ref):
    for k in range(8):
        high, low = split(t_ref[k])
        wz_ref[:128, 256 * k : 256 * k + 256] = high
        wz_ref[128:, 256 * k : 256 * k + 256] = low
        high, low = split(t_ref[k].T)
        wy_ref[0, :, 128 * k : 128 * k + 128] = high
        wy_ref[1, :, 128 * k : 128 * k + 128] = low


def pack(square, first, step):
    tiles = [square[8 * q : 8 * q + 8] for q in range(4)]
    return sum(pltpu.roll(tiles[q], first + step * q, 1) if first + q else tiles[q] for q in range(4))


def widen(x):
    return jnp.concatenate([x, jnp.zeros((128 - x.shape[0], x.shape[1]), F32)], 0)


def unpack_gram(halves):
    return jnp.concatenate([half[32:40, 32 * q : 32 * q + 32] for half in halves for q in range(2)], 0)


def update(core, both_ref, fa, fb, fc):
    rows = [both_ref[0, h] for h in range(2)]
    cols = [both_ref[1, h] for h in range(2)]
    mode_a = jnp.concatenate([jnp.where(core == 0, col[:16], col[16:32]) for col in cols], 0)
    mode_b = jnp.concatenate([jnp.concatenate([row[:16], row[16:32]], 1) for row in rows], 0)
    gram_a, gram_b = (unpack_gram(rows), unpack_gram(cols))
    gram_c = product(fc, fc, (1, 1))
    next_a = descend(fa, gram_b * gram_c, mode_a)
    next_b = descend(fb, gram_a * gram_c, mode_b)
    h_c = gram_a * gram_b
    scale = inverse_norm(h_c)
    return next_a, next_b, fc - scale * product(h_c, fc), scale


def add_mode_c(base, scale, total):
    mode_c = jnp.concatenate([total[:, 64 + 8 * q : 72 + 8 * q] for q in range(4)], 0)
    return base + scale * mode_c


def multiply(fa, fb, wz_ref, wy_ref):
    a_high, a_low = split(fa)
    b_high, b_low = split(fb)
    left = jnp.concatenate([jnp.concatenate([a_high, a_high], 1), jnp.concatenate([a_low, jnp.zeros_like(a_low)], 1)], 0)
    z = product(left, wz_ref[...], precision=None)
    z = z[:32] + z[32:]
    y = product(jnp.concatenate([b_high, b_low], 0), wy_ref[0], precision=None)
    y = y[:32] + y[32:] + product(b_high, wy_ref[1], precision=None)
    lane = lax.broadcasted_iota(jnp.int32, (32, 128), 1)
    part_c = jnp.zeros((32, 128), F32)
    for k in range(8):
        part_c = jnp.where(lane == k, jnp.sum(y[:, 128 * k : 128 * k + 128] * fa, 1, keepdims=True), part_c)
    gram_a = product(fa, widen(fa), (1, 1))
    gram_b = product(fb, widen(fb), (1, 1))
    return y, z, pack(gram_a, 0, 32), pack(gram_b, 0, 32), pack(part_c, 64, 8)


def columns(wide):
    square = (lax.broadcasted_iota(jnp.int32, (8, 8), 0) == lax.broadcasted_iota(jnp.int32, (8, 8), 1)).astype(F32)
    return product(wide, square, (0, 0))


def keep_or_send(core, products, keep_ref, send_ref, gram_ref):
    y, z, gram_a, gram_b, part_c = products
    for block in range(16):
        rows = slice(32 * block, 32 * block + 32)
        z_block = z[:, 128 * block : 128 * block + 128]
        y_block = y[:, 128 * (block % 8) : 128 * (block % 8) + 128]
        keep_ref[rows] = jnp.where(core == 0, z_block, y_block)
        send_ref[rows] = jnp.where(core == 0, y_block, z_block)
    send_ref[512:520] = gram_a
    send_ref[520:528] = part_c
    send_ref[528:536] = part_c
    gram_ref[...] = gram_b


def message(core, fc, both_ref, keep_ref, gram_ref, out_ref):
    size = out_ref.shape[0]

    def write(low, high, gram, slots):
        part_c = both_ref[0, 520:528] + both_ref[1, 520:528]
        lane = lax.broadcasted_iota(jnp.int32, (8, 128), 1)
        for h in range(2):
            tile = jnp.where(lane < 64, pltpu.roll(gram, 64, 1) if h else gram, part_c)
            for n in slots[h]:
                out_ref[n, 0:16] = low[16 * h : 16 * h + 16]
                out_ref[n, 16:32] = high[16 * h : 16 * h + 16]
                out_ref[n, 32:40] = tile

    @pl.when(core == 0)
    def _():
        low, high = (jnp.zeros((32, 128), F32), jnp.zeros((32, 128), F32))
        for k in range(8):
            weight = fc[:, k : k + 1]
            low += weight * (keep_ref[64 * k : 64 * k + 32] + both_ref[1, 64 * k : 64 * k + 32])
            high += weight * (keep_ref[64 * k + 32 : 64 * k + 64] + both_ref[1, 64 * k + 32 : 64 * k + 64])
        write(low, high, both_ref[0, 512:520] + both_ref[1, 512:520], [range(0, size, 2), range(1, size, 2)])

    @pl.when(core == 1)
    def _():
        low, high = (jnp.zeros((32, 128), F32), jnp.zeros((32, 128), F32))
        for k in range(8):
            weight = fc[:, k : k + 1]
            low += weight * both_ref[0, 32 * k : 32 * k + 32]
            high += weight * keep_ref[32 * k : 32 * k + 32]
        write(low, high, gram_ref[...], [range(size // 2), range(size // 2, size)])


def start_kernel(place_ref, t_ref, fa_ref, fb_ref, wz_ref, wy_ref, keep_ref, send_ref, gram_ref):
    prepare(t_ref, wz_ref, wy_ref)
    keep_or_send(place_ref[0], multiply(fa_ref[...], fb_ref[...], wz_ref, wy_ref), keep_ref, send_ref, gram_ref)


def first_kernel(place_ref, fc_ref, both_ref, keep_ref, gram_ref, nc_ref, out_ref):
    fc = columns(fc_ref[...])
    nc_ref[...] = fc
    message(place_ref[0], fc, both_ref, keep_ref, gram_ref, out_ref)


def ring_kernel(got_ref, sum_ref, ring_ref):
    total = got_ref[0]
    for n in range(1, got_ref.shape[0]):
        total += got_ref[n]
    sum_ref[...] = total
    for n in range(ring_ref.shape[0]):
        ring_ref[n] = total[32:]


def factor_kernel(place_ref, both_ref, fa_ref, fb_ref, fc_ref, wz_ref, wy_ref, na_ref, nb_ref, base_ref, scale_ref, keep_ref, send_ref, gram_ref):
    core = place_ref[0]
    fa, fb, base, scale = update(core, both_ref, fa_ref[...], fb_ref[...], fc_ref[...])
    na_ref[...] = fa
    nb_ref[...] = fb
    base_ref[...] = base
    scale_ref[...] = jnp.broadcast_to(scale, (8, 128))
    keep_or_send(core, multiply(fa, fb, wz_ref, wy_ref), keep_ref, send_ref, gram_ref)


def chip_kernel(place_ref, base_ref, scale_ref, both_ref, keep_ref, gram_ref, nc_ref, out_ref):
    fc = add_mode_c(base_ref[...], scale_ref[:1, :1], both_ref[0, 528:536])
    nc_ref[...] = fc
    message(place_ref[0], fc, both_ref, keep_ref, gram_ref, out_ref)


def last_factor_kernel(place_ref, both_ref, fa_ref, fb_ref, fc_ref, na_ref, nb_ref, base_ref, scale_ref):
    fa, fb, base, scale = update(place_ref[0], both_ref, fa_ref[...], fb_ref[...], fc_ref[...])
    na_ref[...] = fa
    nb_ref[...] = fb
    base_ref[...] = base
    scale_ref[...] = jnp.broadcast_to(scale, (8, 128))


def last_c_kernel(total_ref, base_ref, scale_ref, nc_ref):
    nc_ref[...] = add_mode_c(base_ref[...], scale_ref[:1, :1], total_ref[0]).T


def call(kernel, outs, *args):
    shapes = [jax.ShapeDtypeStruct(s, d) for s, d in outs]
    specs = [SMEM if a.dtype == jnp.int32 else VMEM for a in args]
    params = pltpu.CompilerParams(vmem_limit_bytes=16 * 1024 * 1024)
    cost = pl.CostEstimate(flops=100_000_000, bytes_accessed=4_000_000, transcendentals=0)
    return pl.pallas_call(kernel, out_shape=shapes, in_specs=specs, out_specs=[VMEM] * len(shapes), compiler_params=params, cost_estimate=cost)(*args)


A, B, C = (((32, 128), F32), ((32, 256), F32), ((32, 8), F32))
TILE = ((8, 128), F32)
PRODUCTS = [((512, 128), F32), ((536, 128), F32), TILE]
ALL = ("x_hi", "z", "core", "y", "x_lo")


def groups_of(size_z, size_y):
    def at(x_hi, z, core, y, x_lo):
        return (((x_hi * size_z + z) * 2 + core) * size_y + y) * 2 + x_lo

    two, zs, ys = (range(2), range(size_z), range(size_y))
    rings = [[at(h, z, 0, y, l) for h in two for z in zs] for l in two for y in ys]
    rings += [[at(h, z, 1, y, l) for l in two for y in ys] for h in two for z in zs]
    pairs = [[at(h, z, 0, y, l), at(h, z + 1, 0, y, l)] for h in two for z in zs[::2] for y in ys for l in two]
    pairs += [[at(h, z, 1, y, l) for l in two] for z in zs for y in ys for h in two]
    return rings, pairs


def shards(size_z, size_y, tensor, factor_a, factor_b, factor_c):
    fa, fb, fc = (factor_a, factor_b, factor_c)
    place = lax.axis_index("core").reshape(1).astype(jnp.int32)
    rings, pairs = groups_of(size_z, size_y)
    out = ((2 * size_z, 40, 128), F32)
    weights = [((256, 2048), BF16), ((2, 256, 1024), BF16)]
    *weights, keep, send, gram_b = call(start_kernel, weights + PRODUCTS, place, tensor, fa, fb)
    both = lax.all_gather(send, "core")
    fc, sent = call(first_kernel, [C, out], place, fc.T, both, keep, gram_b)
    for step in range(ITERS):
        got = lax.all_to_all(sent, ALL, 0, 0, axis_index_groups=rings)
        sums, ring = call(ring_kernel, [((40, 128), F32), ((2 * size_y, 8, 128), F32)], got)
        ring = lax.all_to_all(ring, ("y", "x_lo"), 0, 0)
        both = lax.all_gather(sums, ALL, axis_index_groups=pairs)
        both = lax.all_gather(both, "core")
        if step < ITERS - 1:
            fa, fb, base, scale, keep, send, gram_b = call(factor_kernel, [A, B, C, TILE] + PRODUCTS, place, both, fa, fb, fc, *weights)
            send = lax.dynamic_update_slice(send, ring.sum(0), (528, 0))
            both = lax.all_gather(send, "core")
            fc, sent = call(chip_kernel, [C, out], place, base, scale, both, keep, gram_b)
        else:
            fa, fb, base, scale = call(last_factor_kernel, [A, B, C, TILE], place, both, fa, fb, fc)
            total = lax.all_gather(ring.sum(0), "core")
            (fc,) = call(last_c_kernel, [((8, 32), F32)], total, base, scale)
    return (fa, fb, fc.T)


def solution(mesh):
    rows, cols = mesh.devices.shape
    devices = mesh.devices.reshape(2, rows // 4, 2, cols // 2, 2)
    fine = Mesh(devices, ("x_hi", "z", "core", "y", "x_lo"))
    row, col = (("x_hi", "z", "core"), ("y", "x_lo"))
    in_specs = (P(None, row, col), P(None, row), P(None, col), P())
    out_specs = (P(None, row), P(None, col), P())
    body = functools.partial(shards, rows // 4, cols // 2)
    return jax.shard_map(body, mesh=fine, in_specs=in_specs, out_specs=out_specs, check_vma=False)
```

```python
import functools

import jax
import jax.numpy as jnp
from jax import lax
from jax.experimental import pallas as pl
from jax.experimental.pallas import tpu as pltpu
from jax.sharding import Mesh, PartitionSpec as P

ITERS = 6

HP = lax.Precision.HIGHEST
F32, BF16 = (jnp.float32, jnp.bfloat16)
VMEM = pl.BlockSpec(memory_space=pltpu.VMEM)
SMEM = pl.BlockSpec(memory_space=pltpu.SMEM)


def product(a, b, contract=(1, 0), precision=HP):
    dims = (((contract[0],), (contract[1],)), ((), ()))
    return lax.dot_general(a, b, dims, precision=precision, preferred_element_type=F32)


def split(x):
    high = x.astype(BF16)
    return high, (x - high.astype(F32)).astype(BF16)


def inverse_norm(matrix):
    return 1.0 / jnp.sqrt(jnp.sum(matrix * matrix, keepdims=True) + 1e-06)


def descend(factor, hessian, contraction):
    return factor - inverse_norm(hessian) * (product(hessian, factor) - contraction)


def prepare(t_ref, wz_ref, wy_ref):
    for k in range(8):
        high, low = split(t_ref[k])
        wz_ref[:128, 256 * k : 256 * k + 256] = high
        wz_ref[128:, 256 * k : 256 * k + 256] = low
        high, low = split(t_ref[k].T)
        wy_ref[0, :, 128 * k : 128 * k + 128] = high
        wy_ref[1, :, 128 * k : 128 * k + 128] = low


def pack(square, first, step):
    tiles = [square[8 * q : 8 * q + 8] for q in range(4)]
    return sum(pltpu.roll(tiles[q], first + step * q, 1) if first + q else tiles[q] for q in range(4))


def widen(x):
    return jnp.concatenate([x, jnp.zeros((128 - x.shape[0], x.shape[1]), F32)], 0)


def unpack_gram(halves):
    return jnp.concatenate([half[32:40, 32 * q : 32 * q + 32] for half in halves for q in range(2)], 0)


def update(core, both_ref, fa, fb, fc):
    rows = [both_ref[0, h] for h in range(2)]
    cols = [both_ref[1, h] for h in range(2)]
    mode_a = jnp.concatenate([jnp.where(core == 0, col[:16], col[16:32]) for col in cols], 0)
    mode_b = jnp.concatenate([jnp.concatenate([row[:16], row[16:32]], 1) for row in rows], 0)
    gram_a, gram_b = (unpack_gram(rows), unpack_gram(cols))
    gram_c = product(fc, fc, (1, 1))
    next_a = descend(fa, gram_b * gram_c, mode_a)
    next_b = descend(fb, gram_a * gram_c, mode_b)
    h_c = gram_a * gram_b
    scale = inverse_norm(h_c)
    return next_a, next_b, fc - scale * product(h_c, fc), scale


def add_mode_c(base, scale, ring_ref):
    total = ring_ref[0]
    for n in range(1, ring_ref.shape[0] // 2):
        total += ring_ref[n]
    mode_c = jnp.concatenate([total[:, 64 + 8 * q : 72 + 8 * q] for q in range(4)], 0)
    return base + scale * mode_c


def multiply(fa, fb, wz_ref, wy_ref):
    a_high, a_low = split(fa)
    b_high, b_low = split(fb)
    left = jnp.concatenate([jnp.concatenate([a_high, a_high], 1), jnp.concatenate([a_low, jnp.zeros_like(a_low)], 1)], 0)
    z = product(left, wz_ref[...], precision=None)
    z = z[:32] + z[32:]
    y = product(jnp.concatenate([b_high, b_low], 0), wy_ref[0], precision=None)
    y = y[:32] + y[32:] + product(b_high, wy_ref[1], precision=None)
    lane = lax.broadcasted_iota(jnp.int32, (32, 128), 1)
    part_c = jnp.zeros((32, 128), F32)
    for k in range(8):
        part_c = jnp.where(lane == k, jnp.sum(y[:, 128 * k : 128 * k + 128] * fa, 1, keepdims=True), part_c)
    gram_a = product(fa, widen(fa), (1, 1))
    gram_b = product(fb, widen(fb), (1, 1))
    return y, z, pack(gram_a, 0, 32), pack(gram_b, 0, 32), pack(part_c, 64, 8)


def message(fc, y, z, gram_a, part_c, sent_ref):
    part_a = jnp.zeros((32, 128), F32)
    part_b = jnp.zeros((32, 256), F32)
    for k in range(8):
        weight = fc[:, k : k + 1]
        part_a += weight * y[:, 128 * k : 128 * k + 128]
        part_b += weight * z[:, 256 * k : 256 * k + 256]
    sent_ref[0:32] = part_b[:, :128]
    sent_ref[32:64] = part_b[:, 128:]
    sent_ref[64:96] = part_a
    sent_ref[96:104] = gram_a
    sent_ref[104:112] = part_c


def start_kernel(t_ref, fa_ref, fb_ref, fc_ref, wz_ref, wy_ref, nc_ref, gram_ref, sent_ref):
    square = (lax.broadcasted_iota(jnp.int32, (8, 8), 0) == lax.broadcasted_iota(jnp.int32, (8, 8), 1)).astype(F32)
    fc = product(fc_ref[...], square, (0, 0))
    nc_ref[...] = fc
    prepare(t_ref, wz_ref, wy_ref)
    y, z, gram_a, gram_b, part_c = multiply(fa_ref[...], fb_ref[...], wz_ref, wy_ref)
    gram_ref[...] = gram_b
    message(fc, y, z, gram_a, part_c, sent_ref)


def chip_kernel(place_ref, both_ref, gram_ref, out_ref):
    first = place_ref[0] == 0
    low = jnp.where(first, both_ref[0, 0:32] + both_ref[1, 0:32], both_ref[0, 64:96])
    high = jnp.where(first, both_ref[0, 32:64] + both_ref[1, 32:64], both_ref[1, 64:96])
    gram = jnp.where(first, both_ref[0, 96:104] + both_ref[1, 96:104], gram_ref[...])
    part_c = both_ref[0, 104:112] + both_ref[1, 104:112]
    lane = lax.broadcasted_iota(jnp.int32, (8, 128), 1)
    size = out_ref.shape[0]
    tiles = [jnp.where(lane < 64, pltpu.roll(gram, 64, 1) if h else gram, part_c) for h in range(2)]

    def write(slots):
        for h in range(2):
            for n in slots[h]:
                out_ref[n, 0:16] = low[16 * h : 16 * h + 16]
                out_ref[n, 16:32] = high[16 * h : 16 * h + 16]
                out_ref[n, 32:40] = tiles[h]

    @pl.when(first)
    def _():
        write([range(0, size, 2), range(1, size, 2)])

    @pl.when(jnp.logical_not(first))
    def _():
        write([range(size // 2), range(size // 2, size)])


def ring_kernel(got_ref, sum_ref, ring_ref):
    total = got_ref[0]
    for n in range(1, got_ref.shape[0]):
        total += got_ref[n]
    sum_ref[...] = total
    for n in range(ring_ref.shape[0]):
        ring_ref[n] = total[32:]


def factor_kernel(place_ref, both_ref, fa_ref, fb_ref, fc_ref, wz_ref, wy_ref, na_ref, nb_ref, gram_ref, base_ref, scale_ref, y_ref, z_ref, packs_ref):
    fa, fb, base, scale = update(place_ref[0], both_ref, fa_ref[...], fb_ref[...], fc_ref[...])
    na_ref[...] = fa
    nb_ref[...] = fb
    base_ref[...] = base
    scale_ref[...] = jnp.broadcast_to(scale, (8, 128))
    y, z, gram_a, gram_b, part_c = multiply(fa, fb, wz_ref, wy_ref)
    y_ref[...] = y
    z_ref[...] = z
    gram_ref[...] = gram_b
    packs_ref[0] = gram_a
    packs_ref[1] = part_c


def send_kernel(ring_ref, base_ref, scale_ref, y_ref, z_ref, packs_ref, nc_ref, sent_ref):
    fc = add_mode_c(base_ref[...], scale_ref[:1, :1], ring_ref)
    nc_ref[...] = fc
    message(fc, y_ref[...], z_ref[...], packs_ref[0], packs_ref[1], sent_ref)


def last_factor_kernel(place_ref, both_ref, fa_ref, fb_ref, fc_ref, na_ref, nb_ref, base_ref, scale_ref):
    fa, fb, base, scale = update(place_ref[0], both_ref, fa_ref[...], fb_ref[...], fc_ref[...])
    na_ref[...] = fa
    nb_ref[...] = fb
    base_ref[...] = base
    scale_ref[...] = jnp.broadcast_to(scale, (8, 128))


def last_c_kernel(ring_ref, base_ref, scale_ref, nc_ref):
    nc_ref[...] = add_mode_c(base_ref[...], scale_ref[:1, :1], ring_ref).T


def call(kernel, outs, *args):
    shapes = [jax.ShapeDtypeStruct(s, d) for s, d in outs]
    specs = [SMEM if a.dtype == jnp.int32 else VMEM for a in args]
    params = pltpu.CompilerParams(vmem_limit_bytes=16 * 1024 * 1024)
    cost = pl.CostEstimate(flops=100_000_000, bytes_accessed=4_000_000, transcendentals=0)
    return pl.pallas_call(kernel, out_shape=shapes, in_specs=specs, out_specs=[VMEM] * len(shapes), compiler_params=params, cost_estimate=cost)(*args)


A, B, C = (((32, 128), F32), ((32, 256), F32), ((32, 8), F32))
TILE, SENT = (((8, 128), F32), ((112, 128), F32))
PRODUCTS = [TILE, ((32, 1024), F32), ((32, 2048), F32), ((2, 8, 128), F32)]
ALL = ("x_hi", "z", "core", "y", "x_lo")


def groups_of(size_z, size_y):
    def at(x_hi, z, core, y, x_lo):
        return (((x_hi * size_z + z) * 2 + core) * size_y + y) * 2 + x_lo

    two, zs, ys = (range(2), range(size_z), range(size_y))
    rings = [[at(h, z, 0, y, l) for h in two for z in zs] for l in two for y in ys]
    rings += [[at(h, z, 1, y, l) for l in two for y in ys] for h in two for z in zs]
    pairs = [[at(h, z, 0, y, l), at(h, z + 1, 0, y, l)] for h in two for z in zs[::2] for y in ys for l in two]
    pairs += [[at(h, z, 1, y, l) for l in two] for z in zs for y in ys for h in two]
    return rings, pairs


def shards(size_z, size_y, tensor, factor_a, factor_b, factor_c):
    fa, fb, fc = (factor_a, factor_b, factor_c)
    place = lax.axis_index("core").reshape(1).astype(jnp.int32)
    rings, pairs = groups_of(size_z, size_y)
    weights = [((256, 2048), BF16), ((2, 256, 1024), BF16)]
    *weights, fc, gram_b, sent = call(start_kernel, weights + [C, TILE, SENT], tensor, fa, fb, fc.T)
    for step in range(ITERS):
        both = lax.all_gather(sent, "core")
        (sent,) = call(chip_kernel, [((2 * size_z, 40, 128), F32)], place, both, gram_b)
        got = lax.all_to_all(sent, ALL, 0, 0, axis_index_groups=rings)
        sums, ring = call(ring_kernel, [((40, 128), F32), ((4 * size_y, 8, 128), F32)], got)
        ring = lax.all_to_all(ring, ("core", "y", "x_lo"), 0, 0)
        both = lax.all_gather(sums, ALL, axis_index_groups=pairs)
        both = lax.all_gather(both, "core")
        if step < ITERS - 1:
            fa, fb, gram_b, *rest = call(factor_kernel, [A, B, TILE, C] + PRODUCTS, place, both, fa, fb, fc, *weights)
            fc, sent = call(send_kernel, [C, SENT], ring, *rest)
        else:
            fa, fb, base, scale = call(last_factor_kernel, [A, B, C, TILE], place, both, fa, fb, fc)
            (fc,) = call(last_c_kernel, [((8, 32), F32)], ring, base, scale)
    return (fa, fb, fc.T)


def solution(mesh):
    rows, cols = mesh.devices.shape
    devices = mesh.devices.reshape(2, rows // 4, 2, cols // 2, 2)
    fine = Mesh(devices, ("x_hi", "z", "core", "y", "x_lo"))
    row, col = (("x_hi", "z", "core"), ("y", "x_lo"))
    in_specs = (P(None, row, col), P(None, row), P(None, col), P())
    out_specs = (P(None, row), P(None, col), P())
    body = functools.partial(shards, rows // 4, cols // 2)
    return jax.shard_map(body, mesh=fine, in_specs=in_specs, out_specs=out_specs, check_vma=False)
```

```python
import functools

import jax
import jax.numpy as jnp
from jax import lax
from jax.experimental import pallas as pl
from jax.experimental.pallas import tpu as pltpu
from jax.sharding import Mesh, PartitionSpec as P

ITERS = 6

HP = lax.Precision.HIGHEST
F32, BF16 = (jnp.float32, jnp.bfloat16)
VMEM = pl.BlockSpec(memory_space=pltpu.VMEM)
SMEM = pl.BlockSpec(memory_space=pltpu.SMEM)


def product(a, b, contract=(1, 0), precision=HP):
    dims = (((contract[0],), (contract[1],)), ((), ()))
    return lax.dot_general(a, b, dims, precision=precision, preferred_element_type=F32)


def split(x):
    high = x.astype(BF16)
    return high, (x - high.astype(F32)).astype(BF16)


def inverse_norm(matrix):
    return 1.0 / jnp.sqrt(jnp.sum(matrix * matrix, keepdims=True) + 1e-06)


def descend(factor, hessian, contraction):
    return factor - inverse_norm(hessian) * (product(hessian, factor) - contraction)


def prepare(t_ref, wz_ref, wy_ref):
    for k in range(8):
        high, low = split(t_ref[k])
        wz_ref[:128, 256 * k : 256 * k + 256] = high
        wz_ref[128:, 256 * k : 256 * k + 256] = low
        high, low = split(t_ref[k].T)
        wy_ref[0, :, 128 * k : 128 * k + 128] = high
        wy_ref[1, :, 128 * k : 128 * k + 128] = low


def pack(square, first, step):
    tiles = [square[8 * q : 8 * q + 8] for q in range(4)]
    return sum(pltpu.roll(tiles[q], first + step * q, 1) if first + q else tiles[q] for q in range(4))


def widen(x):
    return jnp.concatenate([x, jnp.zeros((128 - x.shape[0], x.shape[1]), F32)], 0)


def unpack_gram(halves):
    return jnp.concatenate([half[32:40, 32 * q : 32 * q + 32] for half in halves for q in range(2)], 0)


def update(core, both_ref, fa, fb, fc):
    rows = [both_ref[0, h] for h in range(2)]
    cols = [both_ref[1, h] for h in range(2)]
    mode_a = jnp.concatenate([jnp.where(core == 0, col[:16], col[16:32]) for col in cols], 0)
    mode_b = jnp.concatenate([jnp.concatenate([row[:16], row[16:32]], 1) for row in rows], 0)
    gram_a, gram_b = (unpack_gram(rows), unpack_gram(cols))
    gram_c = product(fc, fc, (1, 1))
    next_a = descend(fa, gram_b * gram_c, mode_a)
    next_b = descend(fb, gram_a * gram_c, mode_b)
    h_c = gram_a * gram_b
    scale = inverse_norm(h_c)
    return next_a, next_b, fc - scale * product(h_c, fc), scale


def add_mode_c(base, scale, ring_ref):
    total = ring_ref[0]
    for n in range(1, ring_ref.shape[0] // 2):
        total += ring_ref[n]
    mode_c = jnp.concatenate([total[:, 64 + 8 * q : 72 + 8 * q] for q in range(4)], 0)
    return base + scale * mode_c


def multiply(fa, fb, wz_ref, wy_ref):
    a_high, a_low = split(fa)
    b_high, b_low = split(fb)
    left = jnp.concatenate([jnp.concatenate([a_high, a_high], 1), jnp.concatenate([a_low, jnp.zeros_like(a_low)], 1)], 0)
    z = product(left, wz_ref[...], precision=None)
    z = z[:32] + z[32:]
    y = product(jnp.concatenate([b_high, b_low], 0), wy_ref[0], precision=None)
    y = y[:32] + y[32:] + product(b_high, wy_ref[1], precision=None)
    lane = lax.broadcasted_iota(jnp.int32, (32, 128), 1)
    part_c = jnp.zeros((32, 128), F32)
    for k in range(8):
        part_c = jnp.where(lane == k, jnp.sum(y[:, 128 * k : 128 * k + 128] * fa, 1, keepdims=True), part_c)
    gram_a = product(fa, widen(fa), (1, 1))
    gram_b = product(fb, widen(fb), (1, 1))
    return y, z, pack(gram_a, 0, 32), pack(gram_b, 0, 32), pack(part_c, 64, 8)


def message(fc, y, z, gram_a, part_c, sent_ref):
    part_a = jnp.zeros((32, 128), F32)
    part_b = jnp.zeros((32, 256), F32)
    for k in range(8):
        weight = fc[:, k : k + 1]
        part_a += weight * y[:, 128 * k : 128 * k + 128]
        part_b += weight * z[:, 256 * k : 256 * k + 256]
    sent_ref[0:32] = part_b[:, :128]
    sent_ref[32:64] = part_b[:, 128:]
    sent_ref[64:96] = part_a
    sent_ref[96:104] = gram_a
    sent_ref[104:112] = part_c


def start_kernel(fa_ref, fb_ref, fc_ref, wz_ref, wy_ref, nc_ref, gram_ref, sent_ref):
    square = (lax.broadcasted_iota(jnp.int32, (8, 8), 0) == lax.broadcasted_iota(jnp.int32, (8, 8), 1)).astype(F32)
    fc = product(fc_ref[...], square, (0, 0))
    nc_ref[...] = fc
    y, z, gram_a, gram_b, part_c = multiply(fa_ref[...], fb_ref[...], wz_ref, wy_ref)
    gram_ref[...] = gram_b
    message(fc, y, z, gram_a, part_c, sent_ref)


def chip_kernel(place_ref, both_ref, gram_ref, out_ref):
    first = place_ref[0] == 0
    low = jnp.where(first, both_ref[0, 0:32] + both_ref[1, 0:32], both_ref[0, 64:96])
    high = jnp.where(first, both_ref[0, 32:64] + both_ref[1, 32:64], both_ref[1, 64:96])
    gram = jnp.where(first, both_ref[0, 96:104] + both_ref[1, 96:104], gram_ref[...])
    part_c = both_ref[0, 104:112] + both_ref[1, 104:112]
    lane = lax.broadcasted_iota(jnp.int32, (8, 128), 1)
    size = out_ref.shape[0]
    tiles = [jnp.where(lane < 64, pltpu.roll(gram, 64, 1) if h else gram, part_c) for h in range(2)]

    def write(slots):
        for h in range(2):
            for n in slots[h]:
                out_ref[n, 0:16] = low[16 * h : 16 * h + 16]
                out_ref[n, 16:32] = high[16 * h : 16 * h + 16]
                out_ref[n, 32:40] = tiles[h]

    @pl.when(first)
    def _():
        write([range(0, size, 2), range(1, size, 2)])

    @pl.when(jnp.logical_not(first))
    def _():
        write([range(size // 2), range(size // 2, size)])


def ring_kernel(got_ref, sum_ref, ring_ref):
    total = got_ref[0]
    for n in range(1, got_ref.shape[0]):
        total += got_ref[n]
    sum_ref[...] = total
    for n in range(ring_ref.shape[0]):
        ring_ref[n] = total[32:]


def factor_kernel(place_ref, both_ref, fa_ref, fb_ref, fc_ref, wz_ref, wy_ref, na_ref, nb_ref, gram_ref, base_ref, scale_ref, y_ref, z_ref, packs_ref):
    fa, fb, base, scale = update(place_ref[0], both_ref, fa_ref[...], fb_ref[...], fc_ref[...])
    na_ref[...] = fa
    nb_ref[...] = fb
    base_ref[...] = base
    scale_ref[...] = jnp.broadcast_to(scale, (8, 128))
    y, z, gram_a, gram_b, part_c = multiply(fa, fb, wz_ref, wy_ref)
    y_ref[...] = y
    z_ref[...] = z
    gram_ref[...] = gram_b
    packs_ref[0] = gram_a
    packs_ref[1] = part_c


def send_kernel(ring_ref, base_ref, scale_ref, y_ref, z_ref, packs_ref, nc_ref, sent_ref):
    fc = add_mode_c(base_ref[...], scale_ref[:1, :1], ring_ref)
    nc_ref[...] = fc
    message(fc, y_ref[...], z_ref[...], packs_ref[0], packs_ref[1], sent_ref)


def last_factor_kernel(place_ref, both_ref, fa_ref, fb_ref, fc_ref, na_ref, nb_ref, base_ref, scale_ref):
    fa, fb, base, scale = update(place_ref[0], both_ref, fa_ref[...], fb_ref[...], fc_ref[...])
    na_ref[...] = fa
    nb_ref[...] = fb
    base_ref[...] = base
    scale_ref[...] = jnp.broadcast_to(scale, (8, 128))


def last_c_kernel(ring_ref, base_ref, scale_ref, nc_ref):
    nc_ref[...] = add_mode_c(base_ref[...], scale_ref[:1, :1], ring_ref).T


def call(kernel, outs, *args):
    shapes = [jax.ShapeDtypeStruct(s, d) for s, d in outs]
    specs = [SMEM if a.dtype == jnp.int32 else VMEM for a in args]
    params = pltpu.CompilerParams(vmem_limit_bytes=16 * 1024 * 1024)
    cost = pl.CostEstimate(flops=100_000_000, bytes_accessed=4_000_000, transcendentals=0)
    return pl.pallas_call(kernel, out_shape=shapes, in_specs=specs, out_specs=[VMEM] * len(shapes), compiler_params=params, cost_estimate=cost)(*args)


A, B, C = (((32, 128), F32), ((32, 256), F32), ((32, 8), F32))
TILE, SENT = (((8, 128), F32), ((112, 128), F32))
PRODUCTS = [TILE, ((32, 1024), F32), ((32, 2048), F32), ((2, 8, 128), F32)]
ALL = ("x_hi", "z", "core", "y", "x_lo")


def groups_of(size_z, size_y):
    def at(x_hi, z, core, y, x_lo):
        return (((x_hi * size_z + z) * 2 + core) * size_y + y) * 2 + x_lo

    two, zs, ys = (range(2), range(size_z), range(size_y))
    rings = [[at(h, z, 0, y, l) for h in two for z in zs] for l in two for y in ys]
    rings += [[at(h, z, 1, y, l) for l in two for y in ys] for h in two for z in zs]
    pairs = [[at(h, z, 0, y, l), at(h, z + 1, 0, y, l)] for h in two for z in zs[::2] for y in ys for l in two]
    pairs += [[at(h, z, 1, y, l) for l in two] for z in zs for y in ys for h in two]
    return rings, pairs


def shards(size_z, size_y, tensor, factor_a, factor_b, factor_c):
    fa, fb, fc = (factor_a, factor_b, factor_c)
    place = lax.axis_index("core").reshape(1).astype(jnp.int32)
    rings, pairs = groups_of(size_z, size_y)
    weights = call(prepare, [((256, 2048), BF16), ((2, 256, 1024), BF16)], tensor)
    fc, gram_b, sent = call(start_kernel, [C, TILE, SENT], fa, fb, fc.T, *weights)
    for step in range(ITERS):
        both = lax.all_gather(sent, "core")
        (sent,) = call(chip_kernel, [((2 * size_z, 40, 128), F32)], place, both, gram_b)
        got = lax.all_to_all(sent, ALL, 0, 0, axis_index_groups=rings)
        sums, ring = call(ring_kernel, [((40, 128), F32), ((4 * size_y, 8, 128), F32)], got)
        ring = lax.all_to_all(ring, ("core", "y", "x_lo"), 0, 0)
        both = lax.all_gather(sums, ALL, axis_index_groups=pairs)
        both = lax.all_gather(both, "core")
        if step < ITERS - 1:
            fa, fb, gram_b, *rest = call(factor_kernel, [A, B, TILE, C] + PRODUCTS, place, both, fa, fb, fc, *weights)
            fc, sent = call(send_kernel, [C, SENT], ring, *rest)
        else:
            fa, fb, base, scale = call(last_factor_kernel, [A, B, C, TILE], place, both, fa, fb, fc)
            (fc,) = call(last_c_kernel, [((8, 32), F32)], ring, base, scale)
    return (fa, fb, fc.T)


def solution(mesh):
    rows, cols = mesh.devices.shape
    devices = mesh.devices.reshape(2, rows // 4, 2, cols // 2, 2)
    fine = Mesh(devices, ("x_hi", "z", "core", "y", "x_lo"))
    row, col = (("x_hi", "z", "core"), ("y", "x_lo"))
    in_specs = (P(None, row, col), P(None, row), P(None, col), P())
    out_specs = (P(None, row), P(None, col), P())
    body = functools.partial(shards, rows // 4, cols // 2)
    return jax.shard_map(body, mesh=fine, in_specs=in_specs, out_specs=out_specs, check_vma=False)
```

```python
import functools

import jax
import jax.numpy as jnp
from jax import lax
from jax.experimental import pallas as pl
from jax.experimental.pallas import tpu as pltpu
from jax.sharding import Mesh, PartitionSpec as P

ITERS = 6

HP = lax.Precision.HIGHEST
F32, BF16 = (jnp.float32, jnp.bfloat16)
VMEM = pl.BlockSpec(memory_space=pltpu.VMEM)
SMEM = pl.BlockSpec(memory_space=pltpu.SMEM)


def product(a, b, contract=(1, 0), precision=HP):
    dims = (((contract[0],), (contract[1],)), ((), ()))
    return lax.dot_general(a, b, dims, precision=precision, preferred_element_type=F32)


def split(x):
    high = x.astype(BF16)
    return high, (x - high.astype(F32)).astype(BF16)


def inverse_norm(matrix):
    return 1.0 / jnp.sqrt(jnp.sum(matrix * matrix, keepdims=True) + 1e-06)


def descend(factor, hessian, contraction):
    return factor - inverse_norm(hessian) * (product(hessian, factor) - contraction)


def prepare(t_ref, wz_ref, wy_ref):
    for k in range(8):
        high, low = split(t_ref[k])
        wz_ref[:128, 256 * k : 256 * k + 256] = high
        wz_ref[128:, 256 * k : 256 * k + 256] = low
        high, low = split(t_ref[k].T)
        wy_ref[0, :, 128 * k : 128 * k + 128] = high
        wy_ref[1, :, 128 * k : 128 * k + 128] = low


def pack(square, first, step):
    tiles = [square[8 * q : 8 * q + 8] for q in range(4)]
    return sum(pltpu.roll(tiles[q], first + step * q, 1) if first + q else tiles[q] for q in range(4))


def widen(x):
    return jnp.concatenate([x, jnp.zeros((128 - x.shape[0], x.shape[1]), F32)], 0)


def unpack_gram(halves):
    return jnp.concatenate([half[32:40, 32 * q : 32 * q + 32] for half in halves for q in range(2)], 0)


def update(core, both_ref, fa, fb, fc):
    rows = [both_ref[0, h] for h in range(2)]
    cols = [both_ref[1, h] for h in range(2)]
    mode_a = jnp.concatenate([jnp.where(core == 0, col[:16], col[16:32]) for col in cols], 0)
    mode_b = jnp.concatenate([jnp.concatenate([row[:16], row[16:32]], 1) for row in rows], 0)
    gram_a, gram_b = (unpack_gram(rows), unpack_gram(cols))
    gram_c = product(fc, fc, (1, 1))
    next_a = descend(fa, gram_b * gram_c, mode_a)
    next_b = descend(fb, gram_a * gram_c, mode_b)
    h_c = gram_a * gram_b
    scale = inverse_norm(h_c)
    return next_a, next_b, fc - scale * product(h_c, fc), scale


def add_mode_c(base, scale, ring_ref):
    total = ring_ref[0]
    for n in range(1, ring_ref.shape[0] // 2):
        total += ring_ref[n]
    mode_c = jnp.concatenate([total[:, 64 + 8 * q : 72 + 8 * q] for q in range(4)], 0)
    return base + scale * mode_c


def multiply(fa, fb, wz_ref, wy_ref):
    a_high, a_low = split(fa)
    b_high, b_low = split(fb)
    left = jnp.concatenate([jnp.concatenate([a_high, a_high], 1), jnp.concatenate([a_low, jnp.zeros_like(a_low)], 1)], 0)
    z = product(left, wz_ref[...], precision=None)
    z = z[:32] + z[32:]
    y = product(jnp.concatenate([b_high, b_low], 0), wy_ref[0], precision=None)
    y = y[:32] + y[32:] + product(b_high, wy_ref[1], precision=None)
    lane = lax.broadcasted_iota(jnp.int32, (32, 128), 1)
    part_c = jnp.zeros((32, 128), F32)
    for k in range(8):
        part_c = jnp.where(lane == k, jnp.sum(y[:, 128 * k : 128 * k + 128] * fa, 1, keepdims=True), part_c)
    gram_a = product(fa, widen(fa), (1, 1))
    gram_b = product(fb, widen(fb), (1, 1))
    return y, z, pack(gram_a, 0, 32), pack(gram_b, 0, 32), pack(part_c, 64, 8)


def message(fc, y, z, gram_a, part_c, sent_ref):
    part_a = jnp.zeros((32, 128), F32)
    part_b = jnp.zeros((32, 256), F32)
    for k in range(8):
        weight = fc[:, k : k + 1]
        part_a += weight * y[:, 128 * k : 128 * k + 128]
        part_b += weight * z[:, 256 * k : 256 * k + 256]
    sent_ref[0:32] = part_b[:, :128]
    sent_ref[32:64] = part_b[:, 128:]
    sent_ref[64:96] = part_a
    sent_ref[96:104] = gram_a
    sent_ref[104:112] = part_c


def start_kernel(fa_ref, fb_ref, fc_ref, wz_ref, wy_ref, nc_ref, gram_ref, sent_ref):
    square = (lax.broadcasted_iota(jnp.int32, (8, 8), 0) == lax.broadcasted_iota(jnp.int32, (8, 8), 1)).astype(F32)
    fc = product(fc_ref[...], square, (0, 0))
    nc_ref[...] = fc
    y, z, gram_a, gram_b, part_c = multiply(fa_ref[...], fb_ref[...], wz_ref, wy_ref)
    gram_ref[...] = gram_b
    message(fc, y, z, gram_a, part_c, sent_ref)


def chip_kernel(place_ref, both_ref, gram_ref, out_ref):
    first = place_ref[0] == 0
    low = jnp.where(first, both_ref[0, 0:32] + both_ref[1, 0:32], both_ref[0, 64:96])
    high = jnp.where(first, both_ref[0, 32:64] + both_ref[1, 32:64], both_ref[1, 64:96])
    gram = jnp.where(first, both_ref[0, 96:104] + both_ref[1, 96:104], gram_ref[...])
    part_c = both_ref[0, 104:112] + both_ref[1, 104:112]
    lane = lax.broadcasted_iota(jnp.int32, (8, 128), 1)
    size = out_ref.shape[0]
    tiles = [jnp.where(lane < 64, pltpu.roll(gram, 64, 1) if h else gram, part_c) for h in range(2)]

    for h in range(2):
        for n in range(h * size // 2, (h + 1) * size // 2):
            out_ref[n, 0:16] = low[16 * h : 16 * h + 16]
            out_ref[n, 16:32] = high[16 * h : 16 * h + 16]
            out_ref[n, 32:40] = tiles[h]


def ring_kernel(got_ref, sum_ref, ring_ref):
    total = got_ref[0]
    for n in range(1, got_ref.shape[0]):
        total += got_ref[n]
    sum_ref[...] = total
    for n in range(ring_ref.shape[0]):
        ring_ref[n] = total[32:]


def factor_kernel(place_ref, both_ref, fa_ref, fb_ref, fc_ref, wz_ref, wy_ref, na_ref, nb_ref, gram_ref, base_ref, scale_ref, y_ref, z_ref, packs_ref):
    fa, fb, base, scale = update(place_ref[0], both_ref, fa_ref[...], fb_ref[...], fc_ref[...])
    na_ref[...] = fa
    nb_ref[...] = fb
    base_ref[...] = base
    scale_ref[...] = jnp.broadcast_to(scale, (8, 128))
    y, z, gram_a, gram_b, part_c = multiply(fa, fb, wz_ref, wy_ref)
    y_ref[...] = y
    z_ref[...] = z
    gram_ref[...] = gram_b
    packs_ref[0] = gram_a
    packs_ref[1] = part_c


def send_kernel(ring_ref, base_ref, scale_ref, y_ref, z_ref, packs_ref, nc_ref, sent_ref):
    fc = add_mode_c(base_ref[...], scale_ref[:1, :1], ring_ref)
    nc_ref[...] = fc
    message(fc, y_ref[...], z_ref[...], packs_ref[0], packs_ref[1], sent_ref)


def last_factor_kernel(place_ref, both_ref, fa_ref, fb_ref, fc_ref, na_ref, nb_ref, base_ref, scale_ref):
    fa, fb, base, scale = update(place_ref[0], both_ref, fa_ref[...], fb_ref[...], fc_ref[...])
    na_ref[...] = fa
    nb_ref[...] = fb
    base_ref[...] = base
    scale_ref[...] = jnp.broadcast_to(scale, (8, 128))


def last_c_kernel(ring_ref, base_ref, scale_ref, nc_ref):
    nc_ref[...] = add_mode_c(base_ref[...], scale_ref[:1, :1], ring_ref).T


def call(kernel, outs, *args):
    shapes = [jax.ShapeDtypeStruct(s, d) for s, d in outs]
    specs = [SMEM if a.dtype == jnp.int32 else VMEM for a in args]
    params = pltpu.CompilerParams(vmem_limit_bytes=16 * 1024 * 1024)
    cost = pl.CostEstimate(flops=100_000_000, bytes_accessed=4_000_000, transcendentals=0)
    return pl.pallas_call(kernel, out_shape=shapes, in_specs=specs, out_specs=[VMEM] * len(shapes), compiler_params=params, cost_estimate=cost)(*args)


A, B, C = (((32, 128), F32), ((32, 256), F32), ((32, 8), F32))
TILE, SENT = (((8, 128), F32), ((112, 128), F32))
PRODUCTS = [TILE, ((32, 1024), F32), ((32, 2048), F32), ((2, 8, 128), F32)]
ALL = ("x_hi", "z", "core", "y", "x_lo")


def groups_of(size_z, size_y):
    def at(x_hi, z, core, y, x_lo):
        return (((x_hi * size_z + z) * 2 + core) * size_y + y) * 2 + x_lo

    two, zs, ys = (range(2), range(size_z), range(size_y))
    rings = [[at(h, z, 0, y, l) for p in two for h in two for z in zs[p::2]] for l in two for y in ys]
    rings += [[at(h, z, 1, y, l) for l in two for y in ys] for h in two for z in zs]
    pairs = [[at(h, z, 0, y, l), at(h, z + 1, 0, y, l)] for h in two for z in zs[::2] for y in ys for l in two]
    pairs += [[at(h, z, 1, y, l) for l in two] for z in zs for y in ys for h in two]
    return rings, pairs


def shards(size_z, size_y, tensor, factor_a, factor_b, factor_c):
    fa, fb, fc = (factor_a, factor_b, factor_c)
    place = lax.axis_index("core").reshape(1).astype(jnp.int32)
    rings, pairs = groups_of(size_z, size_y)
    weights = call(prepare, [((256, 2048), BF16), ((2, 256, 1024), BF16)], tensor)
    fc, gram_b, sent = call(start_kernel, [C, TILE, SENT], fa, fb, fc.T, *weights)
    for step in range(ITERS):
        both = lax.all_gather(sent, "core")
        (sent,) = call(chip_kernel, [((2 * size_z, 40, 128), F32)], place, both, gram_b)
        got = lax.all_to_all(sent, ALL, 0, 0, axis_index_groups=rings)
        sums, ring = call(ring_kernel, [((40, 128), F32), ((4 * size_y, 8, 128), F32)], got)
        ring = lax.all_to_all(ring, ("core", "y", "x_lo"), 0, 0)
        both = lax.all_gather(sums, ALL, axis_index_groups=pairs)
        both = lax.all_gather(both, "core")
        if step < ITERS - 1:
            fa, fb, gram_b, *rest = call(factor_kernel, [A, B, TILE, C] + PRODUCTS, place, both, fa, fb, fc, *weights)
            fc, sent = call(send_kernel, [C, SENT], ring, *rest)
        else:
            fa, fb, base, scale = call(last_factor_kernel, [A, B, C, TILE], place, both, fa, fb, fc)
            (fc,) = call(last_c_kernel, [((8, 32), F32)], ring, base, scale)
    return (fa, fb, fc.T)


def solution(mesh):
    rows, cols = mesh.devices.shape
    devices = mesh.devices.reshape(2, rows // 4, 2, cols // 2, 2)
    fine = Mesh(devices, ("x_hi", "z", "core", "y", "x_lo"))
    row, col = (("x_hi", "z", "core"), ("y", "x_lo"))
    in_specs = (P(None, row, col), P(None, row), P(None, col), P())
    out_specs = (P(None, row), P(None, col), P())
    body = functools.partial(shards, rows // 4, cols // 2)
    return jax.shard_map(body, mesh=fine, in_specs=in_specs, out_specs=out_specs, check_vma=False)
```
